256 devices in a mesh: blk: 16 (over x, y_hi, core), help: 16 (over z, y_lo).
Axes of the slice: x: 4, y: 4 (y_hi: 2, y_lo: 2; y = y_hi * 2 + y_lo), z: 8, core: 2. Of those that a mesh axis runs over, the one named last changes fastest.
Arguments:
- queries: bfloat16 [2048, 8192], P('help', 'blk'), may hold values from -200 to 200
- query_key_value: bfloat16 [2048, 2048], P('help'), may hold values from -8 to 8
- cached_key_value: bfloat16 [32768, 2048], P(('blk', 'help')), may hold values from -6 to 6
- selected: int32 [16, 64, 8], P('help'), may hold values from 0 to 31, as said below
Outputs:
- attended: float32 [2048, 8192], P('help', 'blk')
The draws below stay inside these ranges and needn't reach their ends.
Inputs may be any that keep to these rules, and one draw needn't show every extreme that they name: `selected`: each query block and head selects 8 distinct context blocks, at most one of each run of 2 blocks c * 2 to (c + 1) * 2 - 1.
All inputs are finite; a program needn't handle non-finite values.
Results may differ from the reference program's by a relative error of at most 0.0058.
Values may be sent and summed in bfloat16 or wider, within the bound.
A program may use at most 128 MiB of HBM per device.

```python
import math
import jax
import jax.numpy as jnp
from jax import lax

HEAD_SIZE = 128
QUERY_HEADS = 64
KEY_VALUE_HEADS = 8
BLOCK_TOKENS = 1024
QUERY_GROUP_ROWS = 128
TOPK = 8
KB = 2
QUERY_ROW_COUNT = 2048
QUERY_BLOCK_COUNT = 16
CONTEXT_BLOCKS = 32
CONTEXT_TOKENS = 32768


def common_fields(key):
    base = jax.random.fold_in(key, 7)
    key_a, random_key_second = jax.random.split(base, 2)
    query = jax.random.normal(key_a, (QUERY_ROW_COUNT, QUERY_HEADS, HEAD_SIZE), jnp.float32)
    fresh_state = jnp.clip(jax.random.normal(random_key_second, (QUERY_ROW_COUNT, 2, KEY_VALUE_HEADS, HEAD_SIZE), jnp.float32), -4.0, 4.0)
    query = jnp.clip(query, -6.0, 6.0)
    return (query, fresh_state)


def draw_queries(key, part):
    query, fresh_state = common_fields(key)
    return query.reshape(QUERY_ROW_COUNT, QUERY_HEADS * HEAD_SIZE).astype(jnp.bfloat16)


def draw_query_key_value(key, part):
    query, fresh_state = common_fields(key)
    return fresh_state.reshape(QUERY_ROW_COUNT, 2 * KEY_VALUE_HEADS * HEAD_SIZE).astype(jnp.bfloat16)


def draw_selected(key, part):
    shards = CONTEXT_BLOCKS // KB
    base = jax.random.fold_in(key, 11)
    key_a, random_key_second = jax.random.split(base)
    noise = jax.random.randint(key_a, (QUERY_BLOCK_COUNT, QUERY_HEADS, shards), 0, 64)
    order = jnp.arange(shards, dtype=jnp.int32)
    bias = jnp.where((order == 0) | (order >= shards - 2), 48, 0).astype(jnp.int32)
    score = (noise + bias[None, None, :]) * shards + order[None, None, :]
    values, chosen = lax.top_k(score, TOPK)
    inner_loop = jax.random.randint(random_key_second, (QUERY_BLOCK_COUNT, QUERY_HEADS, TOPK), 0, KB)
    return (chosen.astype(jnp.int32) * KB + inner_loop).astype(jnp.int32)


def level_of(key, shape, cuts, least, high):
    factor_of = 1.0
    for axis_at, shards_of in cuts:
        heights = jax.random.uniform(jax.random.fold_in(jax.random.fold_in(key, 6), axis_at), (shards_of,), jnp.float32, least / len(cuts), high / len(cuts))
        factor_of = factor_of * jnp.repeat(jnp.exp(heights), shape[axis_at] // shards_of).reshape((-1,) + (1,) * (len(shape) - 1 - axis_at))
    return factor_of


def gaussian(stream_key, extent, width, bound, cuts=(), kind=jnp.bfloat16):
    gain = level_of(stream_key, extent, cuts, -0.22, 0.18) if cuts else 1.0
    array = jax.random.normal(stream_key, extent, jnp.float32) * width * gain
    return jnp.minimum(jnp.maximum(array, -bound), bound).astype(kind)


def setup_inputs(seed: int = 0) -> dict:
    seeds = jax.random.split(jax.random.key(seed), 5)
    queries = draw_queries(jax.random.fold_in(seeds[4], 71), 0)
    query_key_value = draw_query_key_value(jax.random.fold_in(seeds[4], 71), 0)
    cached_key_value = gaussian(seeds[2], (CONTEXT_TOKENS, 2 * KEY_VALUE_HEADS * HEAD_SIZE), 1.0, 6.0, ((0, 256),))
    selected = draw_selected(jax.random.fold_in(seeds[4], 71), 0)
    return {"queries": queries, "query_key_value": query_key_value, "cached_key_value": cached_key_value, "selected": selected}


def reference(queries, query_key_value, cached_key_value, selected):
    scale = 1.0 / math.sqrt(HEAD_SIZE)
    head_group = QUERY_HEADS // KEY_VALUE_HEADS
    selection_table = jnp.transpose(cached_key_value.reshape(CONTEXT_BLOCKS, BLOCK_TOKENS, 2, KEY_VALUE_HEADS, HEAD_SIZE), (0, 3, 2, 1, 4))
    fresh_state = query_key_value.reshape(QUERY_BLOCK_COUNT, QUERY_GROUP_ROWS, 2, KEY_VALUE_HEADS, HEAD_SIZE)
    quer = queries.reshape(QUERY_BLOCK_COUNT, QUERY_GROUP_ROWS, QUERY_HEADS, HEAD_SIZE)
    heads_kv = (jnp.arange(QUERY_HEADS) // head_group).astype(jnp.int32)
    causal = jnp.arange(QUERY_GROUP_ROWS)[:, None] >= jnp.arange(QUERY_GROUP_ROWS)[None, :]

    def one_block(args):
        query_block, own, picks = args
        qf = query_block.astype(jnp.float32)
        chosen = selection_table[picks, heads_kv[:, None]]
        key_rows = chosen[:, :, 0].reshape(QUERY_HEADS, TOPK * BLOCK_TOKENS, HEAD_SIZE).astype(jnp.float32)
        vals = chosen[:, :, 1].reshape(QUERY_HEADS, TOPK * BLOCK_TOKENS, HEAD_SIZE).astype(jnp.float32)
        own_k = own[:, 0][:, heads_kv].astype(jnp.float32)
        own_v = own[:, 1][:, heads_kv].astype(jnp.float32)
        far = jnp.einsum('qhd,hkd->hqk', qf, key_rows) * scale
        near = jnp.einsum('qhd,khd->hqk', qf, own_k) * scale
        near = jnp.where(causal[None], near, -jnp.inf)
        scores = jnp.concatenate([far, near], axis=-1)
        best = lax.optimization_barrier(jnp.max(scores, axis=-1, keepdims=True))
        weight = jnp.exp(scores - best)
        total = lax.optimization_barrier(jnp.sum(weight, axis=-1))
        light = lax.optimization_barrier(weight.astype(jnp.bfloat16)).astype(jnp.float32)
        mixed = jnp.einsum('hqk,hkd->hqd', light[..., :TOPK * BLOCK_TOKENS], vals)
        mixed = mixed + jnp.einsum('hqk,khd->hqd', light[..., TOPK * BLOCK_TOKENS:], own_v)
        out = mixed / total[..., None]
        return jnp.transpose(out, (1, 0, 2)).reshape(QUERY_GROUP_ROWS, QUERY_HEADS * HEAD_SIZE).astype(jnp.float32)
    result = lax.map(one_block, (quer, fresh_state, selected))
    return result.reshape(QUERY_ROW_COUNT, QUERY_HEADS * HEAD_SIZE)
```

```python
import math

import jax
import jax.numpy as jnp
from jax import lax
from jax.experimental import pallas as pl
from jax.experimental.pallas import tpu as pltpu
from jax.sharding import PartitionSpec as P

D = 128
R = 128
G = 8
NZ = 8
TOPK = 8
HEADS = 4
PAIRS = 16
PLANE = 16
FAR = -1e9
SCALE = math.log2(math.e) / math.sqrt(D)
MESH = pl.DeviceIdType.MESH
NT = (((1,), (1,)), ((), ()))


def remote(src, dst, send, recv, blk, hlp):
    return pltpu.make_async_remote_copy(
        src_ref=src, dst_ref=dst, send_sem=send, recv_sem=recv,
        device_id={"blk": blk, "help": hlp}, device_id_type=MESH,
    )


def kernel(
    q_ref, kv_ref, sel_ref, own_ref, out_ref,
    vts, kbuf, vbuf, qbuf, selv, sels, ownk, ownv, scores, part, stats, near, nstat,
    out_o, in_o, out_s, in_s,
    loc_sem, k_send, k_recv, v_send, v_recv, f_send, fk_recv, fv_recv,
    q_send, q_recv, s_send, s_recv, o_send, o_recv, t_send, t_recv,
):
    i = lax.axis_index("blk")
    j = lax.axis_index("help")
    g, u = i // 2, i % 2
    z, ylo = j // 2, j % 2
    me = 2 * g + ylo
    right = 2 * ((z + 1) % NZ) + ylo
    left = 2 * ((z + NZ - 1) % NZ) + ylo
    sib = 2 * g + (1 - u)

    def plane_of(t):
        return 2 * (t // 2) + u, 2 * z + t % 2

    gcol = pl.multiple_of(g * D, D)
    own_k_copy = pltpu.make_async_copy(own_ref.at[:, pl.ds(gcol, D)], ownk, loc_sem.at[0])
    own_v_copy = pltpu.make_async_copy(
        own_ref.at[:, pl.ds(pl.multiple_of(G * D + g * D, D), D)], ownv, loc_sem.at[1]
    )
    own_k_copy.start()
    own_v_copy.start()

    barrier = pltpu.get_barrier_semaphore()

    def greet_plane(k, c):
        b, h = plane_of((me + k) % PLANE)
        pl.semaphore_signal(barrier, inc=1, device_id={"blk": b, "help": h}, device_id_type=MESH)
        return c

    def greet_ring(k, c):
        h = 2 * ((z + k) % NZ) + ylo
        pl.semaphore_signal(barrier, inc=1, device_id={"blk": i, "help": h}, device_id_type=MESH)
        return c

    lax.fori_loop(1, PLANE, greet_plane, 0)
    lax.fori_loop(1, NZ, greet_ring, 0)
    pl.semaphore_signal(barrier, inc=1, device_id={"blk": sib, "help": j}, device_id_type=MESH)
    pl.semaphore_wait(barrier, PLANE - 1 + NZ - 1 + 1)

    def q_copy(way, s, half):
        block = (z - (s - 1)) % NZ if way == 0 else (z + (s - 1)) % NZ
        rows = pl.ds(half * (R // 2), R // 2)
        src = q_ref.at[rows, :] if s == 1 else qbuf.at[block, rows, :]
        return remote(
            src, qbuf.at[block, rows, :], q_send.at[way, s - 1, half], q_recv.at[way, s - 1, half],
            i, right if way == 0 else left,
        )

    def q_halves(s):
        return [(w, h) for h in (0, 1) for w in (0, 1) if s < 4 or w == h]

    for w, h in q_halves(1):
        q_copy(w, 1, h).start()

    def k_copy(k):
        t = (me + k) % PLANE
        b, h = plane_of(t)
        col = pl.multiple_of((t // 2) * D, D)
        return remote(
            kv_ref.at[:, pl.ds(col, D)], kbuf.at[i, ylo], k_send.at[k], k_recv.at[me], b, h
        )

    def v_copy(k):
        t = (me + k) % PLANE
        b, h = plane_of(t)
        return remote(vts.at[t // 2], vbuf.at[i, ylo], v_send.at[k], v_recv.at[me], b, h)

    lax.fori_loop(1, PLANE, lambda k, c: (k_copy(k).start(), c)[1], 0)
    for head in range(G):
        vts[head] = jnp.transpose(kv_ref[:, (G + head) * D : (G + head + 1) * D])
    lax.fori_loop(1, PLANE, lambda k, c: (v_copy(k).start(), c)[1], 0)

    def s_copy(k):
        h = 2 * ((z + k) % NZ) + ylo
        rows = pl.ds(pl.multiple_of(g * 8, 8), 8)
        return remote(sel_ref.at[0, rows, :], selv.at[z], s_send.at[k], s_recv.at[z], i, h)

    lax.fori_loop(1, NZ, lambda k, c: (s_copy(k).start(), c)[1], 0)
    selv[z] = sel_ref[0, pl.ds(pl.multiple_of(g * 8, 8), 8), :]
    qbuf[z] = q_ref[...]
    kbuf[i, ylo] = kv_ref[:, pl.ds(gcol, D)]
    vbuf[i, ylo] = vts[g]

    def forward(s):
        pair = 2 * (s // 2) + u
        slot = s % 2
        return (
            remote(kbuf.at[pair, slot], kbuf.at[pair, slot], f_send.at[0, s], fk_recv.at[s], sib, j),
            remote(vbuf.at[pair, slot], vbuf.at[pair, slot], f_send.at[1, s], fv_recv.at[s], sib, j),
        )

    for copy in forward(me):
        copy.start()

    own_k_copy.wait()
    own_v_copy.wait()
    causal = lax.broadcasted_iota(jnp.int32, (R, R), 0) <= lax.broadcasted_iota(jnp.int32, (R, R), 1)
    own_vt = jnp.transpose(ownv[...])
    for h in range(HEADS):
        s = lax.dot_general(ownk[...], q_ref[:, h * D : (h + 1) * D], NT, preferred_element_type=jnp.float32)
        s = jnp.where(causal, s, FAR)
        top = jnp.max(s, axis=0, keepdims=True)
        w = jnp.exp2((s - top) * SCALE)
        nstat[h : h + 1] = top
        nstat[HEADS + h : HEADS + h + 1] = jnp.sum(w, axis=0, keepdims=True)
        near[h] = jnp.dot(own_vt, w.astype(jnp.bfloat16), preferred_element_type=jnp.float32)

    def arrive(k, c):
        s = (me + PLANE - k) % PLANE
        pair = 2 * (s // 2) + u
        slot = s % 2
        to_k, to_v = forward(s)
        remote(kbuf.at[pair, slot], kbuf.at[pair, slot], k_send.at[k], k_recv.at[s], i, j).wait_recv()
        to_k.start()
        remote(vbuf.at[pair, slot], vbuf.at[pair, slot], v_send.at[k], v_recv.at[s], i, j).wait_recv()
        to_v.start()
        return c

    def q_arrived(way, s, half):
        block = (z - s) % NZ if way == 0 else (z + s) % NZ
        rows = pl.ds(half * (R // 2), R // 2)
        remote(
            qbuf.at[block, rows, :], qbuf.at[block, rows, :], q_send.at[way, s - 1, half],
            q_recv.at[way, s - 1, half], i, right,
        ).wait_recv()

    for s, (lo, hi) in zip((1, 2, 3), ((1, 5), (5, 9), (9, 13))):
        lax.fori_loop(lo, hi, arrive, 0)
        ahead = q_halves(s + 1)
        for w, h in q_halves(s):
            q_arrived(w, s, h)
            if (w, h) in ahead:
                q_copy(w, s + 1, h).start()
    lax.fori_loop(13, PLANE, arrive, 0)
    for w, h in q_halves(4):
        q_arrived(w, 4, h)

    def from_sibling(s, c):
        pair = 2 * (s // 2) + (1 - u)
        slot = s % 2
        remote(kbuf.at[pair, slot], kbuf.at[pair, slot], f_send.at[0, s], fk_recv.at[s], sib, j).wait_recv()
        remote(vbuf.at[pair, slot], vbuf.at[pair, slot], f_send.at[1, s], fv_recv.at[s], sib, j).wait_recv()
        return c

    lax.fori_loop(0, PLANE, from_sibling, 0)

    def picks_arrived(k, c):
        zs = (z + NZ - k) % NZ
        remote(selv.at[zs], selv.at[zs], s_send.at[k], s_recv.at[zs], i, j).wait_recv()
        return c

    lax.fori_loop(1, NZ, picks_arrived, 0)
    to_smem = pltpu.make_async_copy(selv, sels, loc_sem.at[2])
    to_smem.start()
    to_smem.wait()

    parity = z // (NZ // 2)

    def attend(b):
        def first(h):
            q = qbuf[b, :, h * D : (h + 1) * D]
            top = jnp.full((1, R), 4 * FAR, jnp.float32)
            for t in range(TOPK):
                c = sels[b, HEADS * u + h, t]
                k = kbuf[c // 2].reshape(2 * R, D)
                s = lax.dot_general(k, q, NT, preferred_element_type=jnp.float32)
                s = s + jnp.where(c % 2 == parity, 0.0, FAR)
                scores[h % 2, t] = s
                top = jnp.maximum(top, jnp.max(s, axis=0, keepdims=True))
            return top

        def second(h, top):
            total = jnp.zeros((1, R), jnp.float32)
            acc = jnp.zeros((D, R), jnp.float32)
            for t in range(TOPK):
                c = sels[b, HEADS * u + h, t]
                w = jnp.exp2((scores[h % 2, t] - top) * SCALE)
                total = total + jnp.sum(w, axis=0, keepdims=True)
                v = jnp.concatenate([vbuf[c // 2, 0], vbuf[c // 2, 1]], axis=1)
                acc = acc + jnp.dot(v, w.astype(jnp.bfloat16), preferred_element_type=jnp.float32)
            part[b, h] = acc
            stats[b, h : h + 1] = top
            stats[b, HEADS + h : HEADS + h + 1] = total

        top = first(0)
        for h in range(HEADS):
            after = first(h + 1) if h + 1 < HEADS else None
            second(h, top)
            top = after

    def merge(a, b):
        (ma, la, oa), (mb, lb, ob) = a, b
        m = jnp.maximum(ma, mb)
        fa, fb = jnp.exp2((ma - m) * SCALE), jnp.exp2((mb - m) * SCALE)
        return m, la * fa + lb * fb, oa * fa + ob * fb

    def mine(b, h):
        return stats[b, h : h + 1], stats[b, HEADS + h : HEADS + h + 1], part[b, h]

    def came(way, s, h):
        c, r = h // 2, h % 2
        return (
            in_s[way, s, c, r : r + 1], in_s[way, s, c, 2 + r : 3 + r],
            in_o[way, s, h].astype(jnp.float32),
        )

    def back(way, s, c):
        heads = pl.ds(2 * c, 2)
        hlp = right if way == 0 else left
        return (
            remote(out_o.at[way, s, heads], in_o.at[way, s, heads], o_send.at[way, s, c], o_recv.at[way, s, c], i, hlp),
            remote(out_s.at[way, s, c], in_s.at[way, s, c], t_send.at[way, s, c], t_recv.at[way, s, c], i, hlp),
        )

    def sends(way, s, c):
        return s >= 1 or c == way

    for s in range(4):
        ahead = (z + 4 - s) % NZ
        behind = z if s == 0 else (z + 4 + s) % NZ
        lax.fori_loop(0, 2, lambda n, c: (attend(jnp.where(n == 0, ahead, behind)), c)[1], 0)
        for c in (0, 1):
            for way in (0, 1):
                if not sends(way, s, c):
                    continue
                if s >= 1 and sends(way, s - 1, c):
                    for copy in back(way, s - 1, c):
                        copy.wait_recv()
                b = ahead if way == 0 or s == 0 else behind
                for h in (2 * c, 2 * c + 1):
                    state = mine(b, h)
                    if s >= 1 and sends(way, s - 1, c):
                        state = merge(state, came(way, s - 1, h))
                    r = h % 2
                    out_s[way, s, c, r : r + 1] = state[0]
                    out_s[way, s, c, 2 + r : 3 + r] = state[1]
                    out_o[way, s, h] = state[2].astype(jnp.bfloat16)
                for copy in back(way, s, c):
                    copy.start()

    for h in range(HEADS):
        part[z, h], stats[z, h : h + 1], stats[z, HEADS + h : HEADS + h + 1] = (
            lambda m: (m[2], m[0], m[1])
        )(merge(mine(z, h), (nstat[h : h + 1], nstat[HEADS + h : HEADS + h + 1], near[h])))
    for c in (0, 1):
        for way in (0, 1):
            for copy in back(way, 3, c):
                copy.wait_recv()
        for h in (2 * c, 2 * c + 1):
            state = merge(merge(mine(z, h), came(0, 3, h)), came(1, 3, h))
            out_ref[:, h * D : (h + 1) * D] = jnp.transpose(state[2] / state[1])

    for s in range(1, 5):
        for w, h in q_halves(s):
            q_copy(w, s, h).wait_send()
    lax.fori_loop(1, PLANE, lambda k, c: (k_copy(k).wait_send(), v_copy(k).wait_send(), c)[2], 0)
    lax.fori_loop(1, NZ, lambda k, c: (s_copy(k).wait_send(), c)[1], 0)
    lax.fori_loop(0, PLANE, lambda k, c: ([x.wait_send() for x in forward(k)], c)[1], 0)
    for s in range(4):
        for c in (0, 1):
            for way in (0, 1):
                if sends(way, s, c):
                    for copy in back(way, s, c):
                        copy.wait_send()


def local(queries, query_key_value, cached_key_value, selected):
    bf16, f32 = jnp.bfloat16, jnp.float32
    dma = pltpu.SemaphoreType.DMA
    vmem = pl.BlockSpec(memory_space=pltpu.VMEM)
    return pl.pallas_call(
        kernel,
        out_shape=jax.ShapeDtypeStruct((R, HEADS * D), f32),
        in_specs=[vmem, vmem, vmem, pl.BlockSpec(memory_space=pl.ANY)],
        out_specs=vmem,
        scratch_shapes=[
            pltpu.VMEM((G, D, R), bf16),
            pltpu.VMEM((PAIRS, 2, R, D), bf16),
            pltpu.VMEM((PAIRS, 2, D, R), bf16),
            pltpu.VMEM((NZ, R, HEADS * D), bf16),
            pltpu.VMEM((NZ, 8, TOPK), jnp.int32),
            pltpu.SMEM((NZ, 8, TOPK), jnp.int32),
            pltpu.VMEM((R, D), bf16),
            pltpu.VMEM((R, D), bf16),
            pltpu.VMEM((2, TOPK, 2 * R, R), f32),
            pltpu.VMEM((NZ, HEADS, D, R), f32),
            pltpu.VMEM((NZ, 2 * HEADS, R), f32),
            pltpu.VMEM((HEADS, D, R), f32),
            pltpu.VMEM((2 * HEADS, R), f32),
            pltpu.VMEM((2, 4, HEADS, D, R), bf16),
            pltpu.VMEM((2, 4, HEADS, D, R), bf16),
            pltpu.VMEM((2, 4, 2, 8, R), f32),
            pltpu.VMEM((2, 4, 2, 8, R), f32),
            dma((3,)),
            dma((PLANE,)), dma((PLANE,)), dma((PLANE,)), dma((PLANE,)),
            dma((2, PLANE)), dma((PLANE,)), dma((PLANE,)),
            dma((2, 4, 2)), dma((2, 4, 2)),
            dma((NZ,)), dma((NZ,)),
            dma((2, 4, 2)), dma((2, 4, 2)), dma((2, 4, 2)), dma((2, 4, 2)),
        ],
        compiler_params=pltpu.CompilerParams(
            collective_id=0, has_side_effects=True, vmem_limit_bytes=40 * 2**20
        ),
    )(queries, cached_key_value, selected, query_key_value)


def solution(mesh):
    in_specs = (P("help", "blk"), P("help", None), P(("blk", "help"), None), P("help", None, None))
    return jax.shard_map(
        local, mesh=mesh, in_specs=in_specs, out_specs=P("help", "blk"), check_vma=False
    )
```

```python
import math

import jax
import jax.numpy as jnp
from jax import lax
from jax.experimental import pallas as pl
from jax.experimental.pallas import tpu as pltpu
from jax.sharding import PartitionSpec as P

D = 128
R = 128
G = 8
NZ = 8
TOPK = 8
HEADS = 4
PAIRS = 16
PLANE = 16
FAR = -1e9
SCALE = math.log2(math.e) / math.sqrt(D)
MESH = pl.DeviceIdType.MESH
NT = (((1,), (1,)), ((), ()))


def remote(src, dst, send, recv, blk, hlp):
    return pltpu.make_async_remote_copy(
        src_ref=src, dst_ref=dst, send_sem=send, recv_sem=recv,
        device_id={"blk": blk, "help": hlp}, device_id_type=MESH,
    )


def kernel(
    q_ref, kv_ref, sel_ref, own_ref, out_ref,
    kvl, kvt, kvbuf, qbuf, sell, selv, sels, ownk, ownv, scores, part, stats, near, nstat,
    out_o, in_o, out_s, in_s,
    loc_sem, k_send, k_recv, f_send, f_recv,
    q_send, q_recv, s_send, s_recv, o_send, o_recv, t_send, t_recv,
):
    i = lax.axis_index("blk")
    j = lax.axis_index("help")
    g, u = i // 2, i % 2
    z, ylo = j // 2, j % 2
    me = 2 * g + ylo
    right = 2 * ((z + 1) % NZ) + ylo
    left = 2 * ((z + NZ - 1) % NZ) + ylo
    sib = 2 * g + (1 - u)

    def plane_of(t):
        return 2 * (t // 2) + u, 2 * z + t % 2

    barrier = pltpu.get_barrier_semaphore()

    def greet(b, h):
        pl.semaphore_signal(barrier, inc=1, device_id={"blk": b, "help": h}, device_id_type=MESH)

    lax.fori_loop(1, PLANE, lambda k, c: (greet(*plane_of((me + k) % PLANE)), c)[1], 0)
    lax.fori_loop(1, NZ, lambda k, c: (greet(i, 2 * ((z + k) % NZ) + ylo), c)[1], 0)
    greet(sib, j)

    gcol = pl.multiple_of(g * D, D)
    gval = pl.multiple_of(G * D + g * D, D)
    loads = [
        pltpu.make_async_copy(src, dst, loc_sem.at[n])
        for n, (src, dst) in enumerate((
            (kv_ref, kvl), (q_ref, qbuf.at[z]), (sel_ref.at[0], sell),
            (own_ref.at[:, pl.ds(gcol, D)], ownk), (own_ref.at[:, pl.ds(gval, D)], ownv),
        ))
    ]
    for copy in loads:
        copy.start()
    for copy in loads:
        copy.wait()
    for head in range(G):
        kvt[head, 0] = kvl[:, head * D : (head + 1) * D]
        kvt[head, 1] = jnp.transpose(kvl[:, (G + head) * D : (G + head + 1) * D])
    selv[z] = jnp.concatenate([sell[...], jnp.zeros((TOPK, D - sell.shape[1]), jnp.int32)], axis=1)
    kvbuf[i, ylo] = kvt[g]
    pl.semaphore_wait(barrier, PLANE - 1 + NZ - 1 + 1)

    def q_copy(way, s, half):
        block = (z - (s - 1)) % NZ if way == 0 else (z + (s - 1)) % NZ
        rows = pl.ds(half * (R // 2), R // 2)
        return remote(
            qbuf.at[block, rows, :], qbuf.at[block, rows, :],
            q_send.at[way, s - 1, half], q_recv.at[way, s - 1, half],
            i, right if way == 0 else left,
        )

    def q_halves(s):
        return [(w, h) for h in (0, 1) for w in (0, 1) if s < 4 or w == h]

    for w, h in q_halves(1):
        q_copy(w, 1, h).start()

    def kv_copy(k):
        t = (me + k) % PLANE
        b, h = plane_of(t)
        return remote(kvt.at[t // 2], kvbuf.at[i, ylo], k_send.at[k], k_recv.at[me], b, h)

    def forward(s):
        pair = 2 * (s // 2) + u
        slot = s % 2
        return remote(kvbuf.at[pair, slot], kvbuf.at[pair, slot], f_send.at[s], f_recv.at[s], sib, j)

    def s_copy(k):
        h = 2 * ((z + k) % NZ) + ylo
        return remote(selv.at[z], selv.at[z], s_send.at[k], s_recv.at[z], i, h)

    lax.fori_loop(1, PLANE, lambda k, c: (kv_copy(k).start(), c)[1], 0)
    lax.fori_loop(1, NZ, lambda k, c: (s_copy(k).start(), c)[1], 0)
    forward(me).start()

    causal = lax.broadcasted_iota(jnp.int32, (R, R), 0) <= lax.broadcasted_iota(jnp.int32, (R, R), 1)
    own_vt = jnp.transpose(ownv[...])
    for h in range(HEADS):
        s = lax.dot_general(
            ownk[...], qbuf[z, :, h * D : (h + 1) * D], NT, preferred_element_type=jnp.float32
        )
        s = jnp.where(causal, s, FAR)
        top = jnp.max(s, axis=0, keepdims=True)
        w = jnp.exp2((s - top) * SCALE)
        nstat[h : h + 1] = top
        nstat[HEADS + h : HEADS + h + 1] = jnp.sum(w, axis=0, keepdims=True)
        near[h] = jnp.dot(own_vt, w.astype(jnp.bfloat16), preferred_element_type=jnp.float32)

    def arrive(k, c):
        s = (me + PLANE - k) % PLANE
        pair = 2 * (s // 2) + u
        slot = s % 2
        remote(kvbuf.at[pair, slot], kvbuf.at[pair, slot], k_send.at[k], k_recv.at[s], sib, j).wait_recv()
        forward(s).start()
        return c

    def q_arrived(way, s, half):
        block = (z - s) % NZ if way == 0 else (z + s) % NZ
        rows = pl.ds(half * (R // 2), R // 2)
        remote(
            qbuf.at[block, rows, :], qbuf.at[block, rows, :], q_send.at[way, s - 1, half],
            q_recv.at[way, s - 1, half], i, right,
        ).wait_recv()

    for s, (lo, hi) in zip((1, 2, 3), ((1, 4), (4, 7), (7, 10))):
        lax.fori_loop(lo, hi, arrive, 0)
        ahead = q_halves(s + 1)
        for w, h in q_halves(s):
            q_arrived(w, s, h)
            if (w, h) in ahead:
                q_copy(w, s + 1, h).start()
    lax.fori_loop(10, PLANE, arrive, 0)
    for w, h in q_halves(4):
        q_arrived(w, 4, h)

    def picks_arrived(k, c):
        zs = (z + NZ - k) % NZ
        remote(selv.at[zs], selv.at[zs], s_send.at[k], s_recv.at[zs], i, right).wait_recv()
        return c

    lax.fori_loop(1, NZ, picks_arrived, 0)
    to_smem = pltpu.make_async_copy(selv, sels, loc_sem.at[0])
    to_smem.start()

    def from_sibling(s, c):
        pair = 2 * (s // 2) + (1 - u)
        slot = s % 2
        remote(kvbuf.at[pair, slot], kvbuf.at[pair, slot], f_send.at[s], f_recv.at[s], sib, j).wait_recv()
        return c

    lax.fori_loop(0, PLANE, from_sibling, 0)
    to_smem.wait()

    parity = z // (NZ // 2)
    lead = HEADS * i

    def attend(b):
        def first(h):
            q = qbuf[b, :, h * D : (h + 1) * D]
            top = jnp.full((1, R), 4 * FAR, jnp.float32)
            for t in range(TOPK):
                c = sels[b, t, lead + h]
                k = jnp.concatenate([kvbuf[c // 2, 0, 0], kvbuf[c // 2, 1, 0]], axis=0)
                s = lax.dot_general(k, q, NT, preferred_element_type=jnp.float32)
                scores[h % 2, t] = s
                bias = jnp.where(c % 2 == parity, 0.0, FAR)
                top = jnp.maximum(top, jnp.max(s, axis=0, keepdims=True) + bias)
            return top

        def second(h, top):
            total = jnp.zeros((1, R), jnp.float32)
            acc = jnp.zeros((D, R), jnp.float32)
            for t in range(TOPK):
                c = sels[b, t, lead + h]
                level = jnp.where(c % 2 == parity, top * SCALE, -FAR)
                w = jnp.exp2(scores[h % 2, t] * SCALE - level)
                total = total + jnp.sum(w, axis=0, keepdims=True)
                v = jnp.concatenate([kvbuf[c // 2, 0, 1], kvbuf[c // 2, 1, 1]], axis=1)
                acc = acc + jnp.dot(v, w.astype(jnp.bfloat16), preferred_element_type=jnp.float32)
            part[b, h] = acc
            stats[b, h : h + 1] = top
            stats[b, HEADS + h : HEADS + h + 1] = total

        top = first(0)
        for h in range(HEADS):
            after = first(h + 1) if h + 1 < HEADS else None
            second(h, top)
            top = after

    def merge(a, b):
        (ma, la, oa), (mb, lb, ob) = a, b
        m = jnp.maximum(ma, mb)
        fa, fb = jnp.exp2((ma - m) * SCALE), jnp.exp2((mb - m) * SCALE)
        return m, la * fa + lb * fb, oa * fa + ob * fb

    def mine(b, h):
        return stats[b, h : h + 1], stats[b, HEADS + h : HEADS + h + 1], part[b, h]

    def came(way, s, h):
        c, r = h // 2, h % 2
        return (
            in_s[way, s, c, r : r + 1], in_s[way, s, c, 2 + r : 3 + r],
            in_o[way, s, h].astype(jnp.float32),
        )

    def back(way, s, c):
        heads = pl.ds(2 * c, 2)
        hlp = jnp.where(way == 0, right, left)
        return (
            remote(out_o.at[way, s, heads], in_o.at[way, s, heads], o_send.at[way, s, c], o_recv.at[way, s, c], i, hlp),
            remote(out_s.at[way, s, c], in_s.at[way, s, c], t_send.at[way, s, c], t_recv.at[way, s, c], i, hlp),
        )

    def give(way, s, c, b):
        for h in (2 * c, 2 * c + 1):
            top, total, acc = mine(b, h)
            r = h % 2
            out_s[way, s, c, r : r + 1] = top
            out_s[way, s, c, 2 + r : 3 + r] = total
            out_o[way, s, h] = acc.astype(jnp.bfloat16)
        for copy in back(way, s, c):
            copy.start()

    def keep(b, h, state):
        stats[b, h : h + 1], stats[b, HEADS + h : HEADS + h + 1], part[b, h] = state

    def turn(n, carry):
        s = (n + 1) // 2
        way = (n + 1) % 2
        b = jnp.where(n == NZ - 1, z, jnp.where(way == 0, z + 4 - s, z + 4 + s) % NZ)
        attend(b)

        @pl.when(n == 0)
        def _():
            for c in (0, 1):
                give(c, 0, c, b)

        @pl.when((n > 0) & (n < NZ - 1))
        def _():
            for c in (0, 1):
                @pl.when((s >= 2) | (way == c))
                def _():
                    for copy in back(way, s - 1, c):
                        copy.wait_recv()
                    for h in (2 * c, 2 * c + 1):
                        keep(b, h, merge(mine(b, h), came(way, s - 1, h)))

                give(way, s, c, b)

        return carry

    lax.fori_loop(0, NZ, turn, 0)

    for h in range(HEADS):
        keep(z, h, merge(mine(z, h), (nstat[h : h + 1], nstat[HEADS + h : HEADS + h + 1], near[h])))
    for c in (0, 1):
        for way in (0, 1):
            for copy in back(way, 3, c):
                copy.wait_recv()
        for h in (2 * c, 2 * c + 1):
            state = merge(merge(mine(z, h), came(0, 3, h)), came(1, 3, h))
            out_ref[:, h * D : (h + 1) * D] = jnp.transpose(state[2] / state[1])

    for s in range(1, 5):
        for w, h in q_halves(s):
            q_copy(w, s, h).wait_send()
    lax.fori_loop(1, PLANE, lambda k, c: (kv_copy(k).wait_send(), c)[1], 0)
    lax.fori_loop(1, NZ, lambda k, c: (s_copy(k).wait_send(), c)[1], 0)
    lax.fori_loop(0, PLANE, lambda k, c: (forward(k).wait_send(), c)[1], 0)
    for s in range(4):
        for c in (0, 1):
            for way in (0, 1):
                if s >= 1 or c == way:
                    for copy in back(way, s, c):
                        copy.wait_send()


def local(queries, query_key_value, cached_key_value, selected):
    bf16, f32 = jnp.bfloat16, jnp.float32
    dma = pltpu.SemaphoreType.DMA
    hbm = pl.BlockSpec(memory_space=pl.ANY)
    return pl.pallas_call(
        kernel,
        out_shape=jax.ShapeDtypeStruct((R, HEADS * D), f32),
        in_specs=[hbm, hbm, hbm, hbm],
        out_specs=pl.BlockSpec(memory_space=pltpu.VMEM),
        scratch_shapes=[
            pltpu.VMEM((R, 2 * G * D), bf16),
            pltpu.VMEM((G, 2, R, D), bf16),
            pltpu.VMEM((PAIRS, 2, 2, R, D), bf16),
            pltpu.VMEM((NZ, R, HEADS * D), bf16),
            pltpu.VMEM((TOPK, PAIRS * HEADS), jnp.int32),
            pltpu.VMEM((NZ, TOPK, D), jnp.int32),
            pltpu.SMEM((NZ, TOPK, D), jnp.int32),
            pltpu.VMEM((R, D), bf16),
            pltpu.VMEM((R, D), bf16),
            pltpu.VMEM((2, TOPK, 2 * R, R), f32),
            pltpu.VMEM((NZ, HEADS, D, R), f32),
            pltpu.VMEM((NZ, 2 * HEADS, R), f32),
            pltpu.VMEM((HEADS, D, R), f32),
            pltpu.VMEM((2 * HEADS, R), f32),
            pltpu.VMEM((2, 4, HEADS, D, R), bf16),
            pltpu.VMEM((2, 4, HEADS, D, R), bf16),
            pltpu.VMEM((2, 4, 2, 8, R), f32),
            pltpu.VMEM((2, 4, 2, 8, R), f32),
            dma((5,)),
            dma((PLANE,)), dma((PLANE,)), dma((PLANE,)), dma((PLANE,)),
            dma((2, 4, 2)), dma((2, 4, 2)),
            dma((NZ,)), dma((NZ,)),
            dma((2, 4, 2)), dma((2, 4, 2)), dma((2, 4, 2)), dma((2, 4, 2)),
        ],
        compiler_params=pltpu.CompilerParams(
            collective_id=0, has_side_effects=True, vmem_limit_bytes=58 * 2**20
        ),
    )(queries, cached_key_value, jnp.transpose(selected, (0, 2, 1)), query_key_value)


def solution(mesh):
    in_specs = (P("help", "blk"), P("help", None), P(("blk", "help"), None), P("help", None, None))
    return jax.shard_map(
        local, mesh=mesh, in_specs=in_specs, out_specs=P("help", "blk"), check_vma=False
    )
```

```python
import math

import jax
import jax.numpy as jnp
from jax import lax
from jax.experimental import pallas as pl
from jax.experimental.pallas import tpu as pltpu
from jax.sharding import PartitionSpec as P

D = 128
R = 128
G = 8
NZ = 8
TOPK = 8
HEADS = 4
PAIRS = 16
PLANE = 16
MESSAGES = 7
FAR = -1e9
SCALE = math.log2(math.e) / math.sqrt(D)
MESH = pl.DeviceIdType.MESH
NT = (((1,), (1,)), ((), ()))


def remote(src, dst, send, recv, blk, hlp):
    return pltpu.make_async_remote_copy(
        src_ref=src, dst_ref=dst, send_sem=send, recv_sem=recv,
        device_id={"blk": blk, "help": hlp}, device_id_type=MESH,
    )


def kernel(
    q_ref, kv_ref, sel_ref, own_ref, out_ref,
    kvl, kvt, kbuf, vbuf, qbuf, sell, selv, sels, ownk, ownv, scores, part, stats, near, nstat,
    out_o, in_o, out_s, in_s,
    loc_sem, k_send, k_recv, f_send, f_recv,
    q_send, q_recv, s_send, s_recv, o_send, o_recv, t_send, t_recv,
):
    i = lax.axis_index("blk")
    j = lax.axis_index("help")
    g, u = i // 2, i % 2
    z, ylo = j // 2, j % 2
    me = 2 * g + ylo
    right = 2 * ((z + 1) % NZ) + ylo
    sib = 2 * g + (1 - u)

    def plane_of(t):
        return 2 * (t // 2) + u, 2 * z + t % 2

    barrier = pltpu.get_barrier_semaphore()

    def greet(b, h):
        pl.semaphore_signal(barrier, inc=1, device_id={"blk": b, "help": h}, device_id_type=MESH)

    lax.fori_loop(1, PLANE, lambda k, c: (greet(*plane_of((me + k) % PLANE)), c)[1], 0)
    lax.fori_loop(1, NZ, lambda k, c: (greet(i, 2 * ((z + k) % NZ) + ylo), c)[1], 0)
    greet(sib, j)

    gcol = pl.multiple_of(g * D, D)
    gval = pl.multiple_of(G * D + g * D, D)
    loads = [
        pltpu.make_async_copy(src, dst, loc_sem.at[n])
        for n, (src, dst) in enumerate((
            (kv_ref, kvl), (q_ref, qbuf.at[z]), (sel_ref.at[0], sell),
            (own_ref.at[:, pl.ds(gcol, D)], ownk), (own_ref.at[:, pl.ds(gval, D)], ownv),
        ))
    ]
    for copy in loads:
        copy.start()
    for copy in loads:
        copy.wait()
    for head in range(G):
        kvt[head, 0] = kvl[:, head * D : (head + 1) * D]
        kvt[head, 1] = jnp.transpose(kvl[:, (G + head) * D : (G + head + 1) * D])
    selv[z] = jnp.concatenate([sell[...], jnp.zeros((TOPK, D - sell.shape[1]), jnp.int32)], axis=1)
    kbuf[i, ylo] = kvt[g, 0]
    vbuf[i, ylo] = kvt[g, 1]
    pl.semaphore_wait(barrier, PLANE - 1 + NZ - 1 + 1)

    def at(d):
        return (z + d + NZ) % NZ

    def q_copy(n, half):
        src, hop = ((0, 1), (0, -1), (0, 2), (0, -2), (-2, 1), (2, -1), (-2, 2), (2, -2))[n]
        part_of = qbuf.at[at(src), pl.ds(half * (R // 2), R // 2), :]
        return remote(part_of, part_of, q_send.at[n, half], q_recv.at[n, half], i, 2 * at(hop) + ylo)

    def q_came(n, half):
        src = (-1, 1, -2, 2, -3, 3, -4, 4)[n]
        part_of = qbuf.at[at(src), pl.ds(half * (R // 2), R // 2), :]
        remote(part_of, part_of, q_send.at[n, half], q_recv.at[n, half], i, right).wait_recv()

    q_all = [(n, half) for half in (0, 1) for n in (2, 3, 0, 1)]
    q_far = [(n, half) for half in (0, 1) for n in (4, 6, 5, 7) if n < 6 or n == 6 + half]
    for n, half in q_all:
        q_copy(n, half).start()

    held = (kbuf, vbuf)

    def kv_copy(k, e):
        t = (me + k) % PLANE
        b, h = plane_of(t)
        return remote(kvt.at[t // 2, e], held[e].at[i, ylo], k_send.at[e, k], k_recv.at[e, me], b, h)

    def forward(s, e):
        block = held[e].at[2 * (s // 2) + u, s % 2]
        return remote(block, block, f_send.at[e, s], f_recv.at[e, s], sib, j)

    def s_copy(k):
        h = 2 * ((z + k) % NZ) + ylo
        return remote(selv.at[z], selv.at[z], s_send.at[k], s_recv.at[z], i, h)

    lax.fori_loop(1, PLANE, lambda k, c: (kv_copy(k, 0).start(), c)[1], 0)
    lax.fori_loop(1, NZ, lambda k, c: (s_copy(k).start(), c)[1], 0)
    lax.fori_loop(1, PLANE, lambda k, c: (kv_copy(k, 1).start(), c)[1], 0)
    for e in (0, 1):
        forward(me, e).start()

    causal = lax.broadcasted_iota(jnp.int32, (R, R), 0) <= lax.broadcasted_iota(jnp.int32, (R, R), 1)
    own_vt = jnp.transpose(ownv[...])
    for h in range(HEADS):
        s = lax.dot_general(
            ownk[...], qbuf[z, :, h * D : (h + 1) * D], NT, preferred_element_type=jnp.float32
        )
        s = jnp.where(causal, s, FAR)
        top = jnp.max(s, axis=0, keepdims=True)
        w = jnp.exp2((s - top) * SCALE)
        nstat[h, 0:1] = top
        nstat[h, 1:2] = jnp.sum(w, axis=0, keepdims=True)
        near[h] = jnp.dot(own_vt, w.astype(jnp.bfloat16), preferred_element_type=jnp.float32)

    for half in (0, 1):
        for n in (2, 3):
            q_came(n, half)
            for m, other in q_far:
                if other == half and m % 2 == n % 2:
                    q_copy(m, half).start()

    def arrive(e):
        def one(k, c):
            s = (me + PLANE - k) % PLANE
            block = held[e].at[2 * (s // 2) + u, s % 2]
            remote(block, block, k_send.at[e, k], k_recv.at[e, s], sib, j).wait_recv()
            forward(s, e).start()
            return c

        lax.fori_loop(1, PLANE, one, 0)

    def from_sibling(e):
        def one(s, c):
            block = held[e].at[2 * (s // 2) + (1 - u), s % 2]
            remote(block, block, f_send.at[e, s], f_recv.at[e, s], sib, j).wait_recv()
            return c

        lax.fori_loop(0, PLANE, one, 0)

    def picks_came(k, c):
        zs = (z + NZ - k) % NZ
        remote(selv.at[zs], selv.at[zs], s_send.at[k], s_recv.at[zs], i, right).wait_recv()
        return c

    lax.fori_loop(1, NZ, picks_came, 0)
    to_smem = pltpu.make_async_copy(selv, sels, loc_sem.at[0])
    to_smem.start()
    arrive(0)
    for n, half in q_all + q_far:
        if n not in (2, 3):
            q_came(n, half)
    to_smem.wait()
    from_sibling(0)

    parity = z // (NZ // 2)
    lead = HEADS * i

    def score(b, carry):
        for h in range(HEADS):
            q = qbuf[b, :, h * D : (h + 1) * D]
            top = jnp.full((1, R), 4 * FAR, jnp.float32)
            for t in range(TOPK):
                c = sels[b, t, lead + h]
                k = kbuf[c // 2].reshape(2 * R, D)
                s = lax.dot_general(k, q, NT, preferred_element_type=jnp.float32)
                scores[b, h, t] = s
                bias = jnp.where(c % 2 == parity, 0.0, FAR)
                top = jnp.maximum(top, jnp.max(s, axis=0, keepdims=True) + bias)
            stats[b, h, 0:1] = top
        return carry

    lax.fori_loop(0, NZ, score, 0)
    arrive(1)
    from_sibling(1)

    def attend(b, h):
        top = stats[b, h, 0:1]
        total = jnp.zeros((1, R), jnp.float32)
        acc = jnp.zeros((D, R), jnp.float32)
        for t in range(TOPK):
            c = sels[b, t, lead + h]
            level = jnp.where(c % 2 == parity, top * SCALE, -FAR)
            w = jnp.exp2(scores[b, h, t] * SCALE - level)
            total = total + jnp.sum(w, axis=0, keepdims=True)
            v = jnp.concatenate([vbuf[c // 2, 0], vbuf[c // 2, 1]], axis=1)
            acc = acc + jnp.dot(v, w.astype(jnp.bfloat16), preferred_element_type=jnp.float32)
        part[b, h] = acc
        stats[b, h, 1:2] = total

    def merge(a, b):
        (ma, la, oa), (mb, lb, ob) = a, b
        m = jnp.maximum(ma, mb)
        fa, fb = jnp.exp2((ma - m) * SCALE), jnp.exp2((mb - m) * SCALE)
        return m, la * fa + lb * fb, oa * fa + ob * fb

    def mine(b, h):
        return stats[b, h, 0:1], stats[b, h, 1:2], part[b, h]

    def came(n, h):
        return in_s[n, h, 0:1], in_s[n, h, 1:2], in_o[n, h].astype(jnp.float32)

    def back(n, c, hop):
        heads = pl.ds(2 * c, 2)
        hlp = 2 * at(hop) + ylo
        return (
            remote(out_o.at[n, heads], in_o.at[n, heads], o_send.at[n, c], o_recv.at[n, c], i, hlp),
            remote(out_s.at[n, heads], in_s.at[n, heads], t_send.at[n, c], t_recv.at[n, c], i, hlp),
        )

    def landed(n, c):
        for copy in back(n, c, 1):
            copy.wait_recv()

    def give(n, c, hop, b, others=()):
        for e in (0, 1):
            h = 2 * c + e
            state = mine(b, h)
            for other in others:
                state = merge(state, came(other, h))
            out_s[n, h, 0:1] = state[0]
            out_s[n, h, 1:2] = state[1]
            out_o[n, h] = state[2].astype(jnp.bfloat16)
        for copy in back(n, c, hop):
            copy.start()

    order = (4, 3, -3, 1, 2, -2, -1, 0)
    messages = {1: (1, 1), 2: (2, -1), 3: (3, 1), 4: (5, 2), 5: (6, -2), 6: (4, -1)}

    def turn(m, carry):
        n, c = m // 2, m % 2
        b = z
        for at_turn, d in enumerate(order):
            b = jnp.where(n == at_turn, at(d), b)
        for e in (0, 1):
            attend(b, 2 * c + e)
        for side in (0, 1):
            @pl.when((n == 0) & (c == side))
            def _(side=side):
                give(0, side, 2 - 4 * side, b)

        for at_turn, (message, hop) in messages.items():
            @pl.when(n == at_turn)
            def _(message=message, hop=hop):
                if message >= 5:
                    side = message - 5
                    landed(message - 4, c)

                    @pl.when(c == side)
                    def _():
                        landed(0, side)
                        give(message, side, hop, b, (message - 4, 0))

                    @pl.when(c != side)
                    def _():
                        give(message, 1 - side, hop, b, (message - 4,))
                else:
                    give(message, c, hop, b)

        return carry

    lax.fori_loop(0, 2 * NZ, turn, 0)

    for c in (0, 1):
        for n in (3, 5, 6, 4):
            landed(n, c)
        for h in (2 * c, 2 * c + 1):
            state = merge(mine(z, h), (nstat[h, 0:1], nstat[h, 1:2], near[h]))
            for n in (3, 5, 6, 4):
                state = merge(state, came(n, h))
            out_ref[:, h * D : (h + 1) * D] = jnp.transpose(state[2] / state[1])

    for n, half in q_all + q_far:
        q_copy(n, half).wait_send()
    for e in (0, 1):
        lax.fori_loop(1, PLANE, lambda k, c: (kv_copy(k, e).wait_send(), c)[1], 0)
        lax.fori_loop(0, PLANE, lambda k, c: (forward(k, e).wait_send(), c)[1], 0)
    lax.fori_loop(1, NZ, lambda k, c: (s_copy(k).wait_send(), c)[1], 0)
    for c in (0, 1):
        for n in range(MESSAGES):
            for copy in back(n, c, 1):
                copy.wait_send()


def local(queries, query_key_value, cached_key_value, selected):
    bf16, f32 = jnp.bfloat16, jnp.float32
    dma = pltpu.SemaphoreType.DMA
    hbm = pl.BlockSpec(memory_space=pl.ANY)
    return pl.pallas_call(
        kernel,
        out_shape=jax.ShapeDtypeStruct((R, HEADS * D), f32),
        in_specs=[hbm, hbm, hbm, hbm],
        out_specs=pl.BlockSpec(memory_space=pltpu.VMEM),
        scratch_shapes=[
            pltpu.VMEM((R, 2 * G * D), bf16),
            pltpu.VMEM((G, 2, R, D), bf16),
            pltpu.VMEM((PAIRS, 2, R, D), bf16),
            pltpu.VMEM((PAIRS, 2, D, R), bf16),
            pltpu.VMEM((NZ, R, HEADS * D), bf16),
            pltpu.VMEM((TOPK, PAIRS * HEADS), jnp.int32),
            pltpu.VMEM((NZ, TOPK, D), jnp.int32),
            pltpu.SMEM((NZ, TOPK, D), jnp.int32),
            pltpu.VMEM((R, D), bf16),
            pltpu.VMEM((R, D), bf16),
            pltpu.VMEM((NZ, HEADS, TOPK, 2 * R, R), f32),
            pltpu.VMEM((NZ, HEADS, D, R), f32),
            pltpu.VMEM((NZ, HEADS, 8, R), f32),
            pltpu.VMEM((HEADS, D, R), f32),
            pltpu.VMEM((HEADS, 8, R), f32),
            pltpu.VMEM((MESSAGES, HEADS, D, R), bf16),
            pltpu.VMEM((MESSAGES, HEADS, D, R), bf16),
            pltpu.VMEM((MESSAGES, HEADS, 8, R), f32),
            pltpu.VMEM((MESSAGES, HEADS, 8, R), f32),
            dma((5,)),
            dma((2, PLANE)), dma((2, PLANE)), dma((2, PLANE)), dma((2, PLANE)),
            dma((8, 2)), dma((8, 2)),
            dma((NZ,)), dma((NZ,)),
            dma((MESSAGES, 2)), dma((MESSAGES, 2)), dma((MESSAGES, 2)), dma((MESSAGES, 2)),
        ],
        compiler_params=pltpu.CompilerParams(
            collective_id=0, has_side_effects=True, vmem_limit_bytes=58 * 2**20
        ),
    )(queries, cached_key_value, jnp.transpose(selected, (0, 2, 1)), query_key_value)


def solution(mesh):
    in_specs = (P("help", "blk"), P("help", None), P(("blk", "help"), None), P("help", None, None))
    return jax.shard_map(
        local, mesh=mesh, in_specs=in_specs, out_specs=P("help", "blk"), check_vma=False
    )
```

```python
import math

import jax
import jax.numpy as jnp
from jax import lax
from jax.experimental import pallas as pl
from jax.experimental.pallas import tpu as pltpu
from jax.sharding import PartitionSpec as P

D = 128
R = 128
G = 8
NZ = 8
TOPK = 8
HEADS = 4
PAIRS = 16
PLANE = 16
PIECES = 4
FAR = -1e9
SCALE = math.log2(math.e) / math.sqrt(D)
MESH = pl.DeviceIdType.MESH
NT = (((1,), (1,)), ((), ()))


def remote(src, dst, send, recv, blk, hlp):
    return pltpu.make_async_remote_copy(
        src_ref=src, dst_ref=dst, send_sem=send, recv_sem=recv,
        device_id={"blk": blk, "help": hlp}, device_id_type=MESH,
    )


def kernel(
    q_ref, kv_ref, sel_ref, own_ref, out_ref,
    kvl, kvt, kbuf, vbuf, qbuf, sell, selv, sels, ownk, ownv, scores, part, stats, near, nstat,
    out_o, in_o, out_s, in_s,
    loc_sem, k_send, k_recv, f_send, f_recv,
    q_send, q_recv, s_send, s_recv, o_send, o_recv, t_send, t_recv,
):
    i = lax.axis_index("blk")
    j = lax.axis_index("help")
    g, u = i // 2, i % 2
    z, ylo = j // 2, j % 2
    me = 2 * g + ylo
    right = 2 * ((z + 1) % NZ) + ylo
    sib = 2 * g + (1 - u)

    def plane_of(t):
        return 2 * (t // 2) + u, 2 * z + t % 2

    barrier = pltpu.get_barrier_semaphore()

    def greet(b, h):
        pl.semaphore_signal(barrier, inc=1, device_id={"blk": b, "help": h}, device_id_type=MESH)

    lax.fori_loop(1, PLANE, lambda k, c: (greet(*plane_of((me + k) % PLANE)), c)[1], 0)
    lax.fori_loop(1, NZ, lambda k, c: (greet(i, 2 * ((z + k) % NZ) + ylo), c)[1], 0)
    greet(sib, j)

    gcol = pl.multiple_of(g * D, D)
    gval = pl.multiple_of(G * D + g * D, D)
    loads = [
        pltpu.make_async_copy(src, dst, loc_sem.at[n])
        for n, (src, dst) in enumerate((
            (kv_ref, kvl), (q_ref, qbuf.at[z]), (sel_ref.at[0], sell),
            (own_ref.at[:, pl.ds(gcol, D)], ownk), (own_ref.at[:, pl.ds(gval, D)], ownv),
        ))
    ]
    for copy in loads:
        copy.start()
    for copy in loads:
        copy.wait()
    for head in range(G):
        kvt[head, 0] = kvl[:, head * D : (head + 1) * D]
        kvt[head, 1] = jnp.transpose(kvl[:, (G + head) * D : (G + head + 1) * D])
    selv[z] = jnp.concatenate([sell[...], jnp.zeros((TOPK, D - sell.shape[1]), jnp.int32)], axis=1)
    kbuf[i, ylo] = kvt[g, 0]
    vbuf[i, ylo] = kvt[g, 1]
    pl.semaphore_wait(barrier, PLANE - 1 + NZ - 1 + 1)

    def at(d):
        return (z + d + NZ) % NZ

    def q_piece(block, p):
        return qbuf.at[at(block), pl.ds(p * (R // PIECES), R // PIECES), :]

    def q_copy(way, s, p):
        part_of = q_piece((s - 1) * (2 * way - 1), p)
        return remote(
            part_of, part_of, q_send.at[way, s - 1, p], q_recv.at[way, s - 1, p], i, 2 * at(1 - 2 * way) + ylo
        )

    def q_came(way, s, p):
        part_of = q_piece(s * (2 * way - 1), p)
        remote(part_of, part_of, q_send.at[way, s - 1, p], q_recv.at[way, s - 1, p], i, right).wait_recv()

    def q_steps(s):
        return [(w, p) for p in range(PIECES) for w in (0, 1) if s < 4 or p // (PIECES // 2) == w]

    def q_pass_on(s):
        for w, p in q_steps(s):
            q_came(w, s, p)
            if (w, p) in q_steps(s + 1):
                q_copy(w, s + 1, p).start()

    for w, p in q_steps(1):
        q_copy(w, 1, p).start()

    held = (kbuf, vbuf)

    def kv_copy(k, e):
        t = (me + k) % PLANE
        b, h = plane_of(t)
        return remote(kvt.at[t // 2, e], held[e].at[i, ylo], k_send.at[e, k], k_recv.at[e, me], b, h)

    def forward(s, e):
        block = held[e].at[2 * (s // 2) + u, s % 2]
        return remote(block, block, f_send.at[e, s], f_recv.at[e, s], sib, j)

    def s_copy(k):
        h = 2 * ((z + k) % NZ) + ylo
        return remote(selv.at[z], selv.at[z], s_send.at[k], s_recv.at[z], i, h)

    lax.fori_loop(1, PLANE, lambda k, c: (kv_copy(k, 0).start(), c)[1], 0)
    lax.fori_loop(1, NZ, lambda k, c: (s_copy(k).start(), c)[1], 0)
    lax.fori_loop(1, PLANE, lambda k, c: (kv_copy(k, 1).start(), c)[1], 0)
    for e in (0, 1):
        forward(me, e).start()

    causal = lax.broadcasted_iota(jnp.int32, (R, R), 0) <= lax.broadcasted_iota(jnp.int32, (R, R), 1)
    own_vt = jnp.transpose(ownv[...])
    for h in range(HEADS):
        s = lax.dot_general(
            ownk[...], qbuf[z, :, h * D : (h + 1) * D], NT, preferred_element_type=jnp.float32
        )
        s = jnp.where(causal, s, FAR)
        top = jnp.max(s, axis=0, keepdims=True)
        w = jnp.exp2((s - top) * SCALE)
        nstat[h, 0:1] = top
        nstat[h, 1:2] = jnp.sum(w, axis=0, keepdims=True)
        near[h] = jnp.dot(own_vt, w.astype(jnp.bfloat16), preferred_element_type=jnp.float32)

    def arrive(e):
        def one(k, c):
            s = (me + PLANE - k) % PLANE
            block = held[e].at[2 * (s // 2) + u, s % 2]
            remote(block, block, k_send.at[e, k], k_recv.at[e, s], sib, j).wait_recv()
            forward(s, e).start()
            return c

        lax.fori_loop(1, PLANE, one, 0)

    def from_sibling(e):
        def one(s, c):
            block = held[e].at[2 * (s // 2) + (1 - u), s % 2]
            remote(block, block, f_send.at[e, s], f_recv.at[e, s], sib, j).wait_recv()
            return c

        lax.fori_loop(0, PLANE, one, 0)

    def picks_came(k, c):
        zs = (z + NZ - k) % NZ
        remote(selv.at[zs], selv.at[zs], s_send.at[k], s_recv.at[zs], i, right).wait_recv()
        return c

    q_pass_on(1)
    lax.fori_loop(1, NZ, picks_came, 0)
    to_smem = pltpu.make_async_copy(selv, sels, loc_sem.at[0])
    to_smem.start()
    q_pass_on(2)
    arrive(0)
    q_pass_on(3)
    to_smem.wait()
    from_sibling(0)

    parity = z // (NZ // 2)
    lead = HEADS * i

    def score(b, carry):
        for h in range(HEADS):
            q = qbuf[b, :, h * D : (h + 1) * D]
            top = jnp.full((1, R), 4 * FAR, jnp.float32)
            for t in range(TOPK):
                c = sels[b, t, lead + h]
                k = kbuf[c // 2].reshape(2 * R, D)
                s = lax.dot_general(k, q, NT, preferred_element_type=jnp.float32)
                scores[b, h, t] = s
                bias = jnp.where(c % 2 == parity, 0.0, FAR)
                top = jnp.maximum(top, jnp.max(s, axis=0, keepdims=True) + bias)
            stats[b, h, 0:1] = top
        return carry

    lax.fori_loop(0, NZ - 1, lambda n, c: score((z + 5 + n) % NZ, c), 0)
    arrive(1)
    for w, p in q_steps(4):
        q_came(w, 4, p)
    score(at(4), 0)
    from_sibling(1)

    def attend(b, h):
        top = stats[b, h, 0:1]
        total = jnp.zeros((1, R), jnp.float32)
        acc = jnp.zeros((D, R), jnp.float32)
        for t in range(TOPK):
            c = sels[b, t, lead + h]
            level = jnp.where(c % 2 == parity, top * SCALE, -FAR)
            w = jnp.exp2(scores[b, h, t] * SCALE - level)
            total = total + jnp.sum(w, axis=0, keepdims=True)
            v = jnp.concatenate([vbuf[c // 2, 0], vbuf[c // 2, 1]], axis=1)
            acc = acc + jnp.dot(v, w.astype(jnp.bfloat16), preferred_element_type=jnp.float32)
        part[b, h] = acc
        stats[b, h, 1:2] = total

    def merge(a, b):
        (ma, la, oa), (mb, lb, ob) = a, b
        m = jnp.maximum(ma, mb)
        fa, fb = jnp.exp2((ma - m) * SCALE), jnp.exp2((mb - m) * SCALE)
        return m, la * fa + lb * fb, oa * fa + ob * fb

    def mine(b, h):
        return stats[b, h, 0:1], stats[b, h, 1:2], part[b, h]

    def came(way, s, h):
        return in_s[way, s, h, 0:1], in_s[way, s, h, 1:2], in_o[way, s, h].astype(jnp.float32)

    def back(way, s, h):
        hlp = 2 * ((z + 1 + (NZ - 2) * way) % NZ) + ylo
        return (
            remote(out_o.at[way, s, h], in_o.at[way, s, h], o_send.at[way, s, h], o_recv.at[way, s, h], i, hlp),
            remote(out_s.at[way, s, h], in_s.at[way, s, h], t_send.at[way, s, h], t_recv.at[way, s, h], i, hlp),
        )

    def landed(way, s, h):
        for copy in back(way, s, h):
            copy.wait_recv()

    def give(way, s, h, state):
        out_s[way, s, h, 0:1] = state[0]
        out_s[way, s, h, 1:2] = state[1]
        out_o[way, s, h] = state[2].astype(jnp.bfloat16)
        for copy in back(way, s, h):
            copy.start()

    def turn(m, carry):
        n, c = m // 2, m % 2
        s = (n + 1) // 2
        way = (n + 1) % 2
        b = jnp.where(n == NZ - 1, z, jnp.where(way == 0, z + 4 - s, z + 4 + s) % NZ)
        for e in (0, 1):
            attend(b, 2 * c + e)

        @pl.when(n == 0)
        def _():
            for e in (0, 1):
                give(c, 0, 2 * c + e, mine(b, 2 * c + e))

        @pl.when(((n == 1) | (n == 2)) & (c != way))
        def _():
            for e in (0, 1):
                give(way, s, 2 * c + e, mine(b, 2 * c + e))

        @pl.when((n < NZ - 1) & ((n > 2) | ((n > 0) & (c == way))))
        def _():
            for e in (0, 1):
                landed(way, s - 1, 2 * c + e)
                give(way, s, 2 * c + e, merge(mine(b, 2 * c + e), came(way, s - 1, 2 * c + e)))

        return carry

    lax.fori_loop(0, 2 * NZ, turn, 0)

    for h in range(HEADS):
        state = merge(mine(z, h), (nstat[h, 0:1], nstat[h, 1:2], near[h]))
        for way in (0, 1):
            landed(way, 3, h)
            state = merge(state, came(way, 3, h))
        out_ref[:, h * D : (h + 1) * D] = jnp.transpose(state[2] / state[1])

    for s in range(1, 5):
        for w, p in q_steps(s):
            q_copy(w, s, p).wait_send()
    for e in (0, 1):
        lax.fori_loop(1, PLANE, lambda k, c: (kv_copy(k, e).wait_send(), c)[1], 0)
        lax.fori_loop(0, PLANE, lambda k, c: (forward(k, e).wait_send(), c)[1], 0)
    lax.fori_loop(1, NZ, lambda k, c: (s_copy(k).wait_send(), c)[1], 0)
    for s in range(4):
        for way in (0, 1):
            for h in range(HEADS):
                if s > 0 or h // 2 == way:
                    for copy in back(way, s, h):
                        copy.wait_send()


def local(queries, query_key_value, cached_key_value, selected):
    bf16, f32 = jnp.bfloat16, jnp.float32
    dma = pltpu.SemaphoreType.DMA
    hbm = pl.BlockSpec(memory_space=pl.ANY)
    return pl.pallas_call(
        kernel,
        out_shape=jax.ShapeDtypeStruct((R, HEADS * D), f32),
        in_specs=[hbm, hbm, hbm, hbm],
        out_specs=pl.BlockSpec(memory_space=pltpu.VMEM),
        scratch_shapes=[
            pltpu.VMEM((R, 2 * G * D), bf16),
            pltpu.VMEM((G, 2, R, D), bf16),
            pltpu.VMEM((PAIRS, 2, R, D), bf16),
            pltpu.VMEM((PAIRS, 2, D, R), bf16),
            pltpu.VMEM((NZ, R, HEADS * D), bf16),
            pltpu.VMEM((TOPK, PAIRS * HEADS), jnp.int32),
            pltpu.VMEM((NZ, TOPK, D), jnp.int32),
            pltpu.SMEM((NZ, TOPK, D), jnp.int32),
            pltpu.VMEM((R, D), bf16),
            pltpu.VMEM((R, D), bf16),
            pltpu.VMEM((NZ, HEADS, TOPK, 2 * R, R), f32),
            pltpu.VMEM((NZ, HEADS, D, R), f32),
            pltpu.VMEM((NZ, HEADS, 8, R), f32),
            pltpu.VMEM((HEADS, D, R), f32),
            pltpu.VMEM((HEADS, 8, R), f32),
            pltpu.VMEM((2, 4, HEADS, D, R), bf16),
            pltpu.VMEM((2, 4, HEADS, D, R), bf16),
            pltpu.VMEM((2, 4, HEADS, 8, R), f32),
            pltpu.VMEM((2, 4, HEADS, 8, R), f32),
            dma((5,)),
            dma((2, PLANE)), dma((2, PLANE)), dma((2, PLANE)), dma((2, PLANE)),
            dma((2, 4, PIECES)), dma((2, 4, PIECES)),
            dma((NZ,)), dma((NZ,)),
            dma((2, 4, HEADS)), dma((2, 4, HEADS)), dma((2, 4, HEADS)), dma((2, 4, HEADS)),
        ],
        compiler_params=pltpu.CompilerParams(
            collective_id=0, has_side_effects=True, vmem_limit_bytes=58 * 2**20
        ),
    )(queries, cached_key_value, jnp.transpose(selected, (0, 2, 1)), query_key_value)


def solution(mesh):
    in_specs = (P("help", "blk"), P("help", None), P(("blk", "help"), None), P("help", None, None))
    return jax.shard_map(
        local, mesh=mesh, in_specs=in_specs, out_specs=P("help", "blk"), check_vma=False
    )
```

```python
import math

import jax
import jax.numpy as jnp
from jax import lax
from jax.experimental import pallas as pl
from jax.experimental.pallas import tpu as pltpu
from jax.sharding import PartitionSpec as P

D = 128
R = 128
G = 8
NZ = 8
TOPK = 8
HEADS = 4
PAIRS = 16
PLANE = 16
PIECES = 4
FAR = -1e9
SCALE = math.log2(math.e) / math.sqrt(D)
MESH = pl.DeviceIdType.MESH
NT = (((1,), (1,)), ((), ()))


def remote(src, dst, send, recv, blk, hlp):
    return pltpu.make_async_remote_copy(
        src_ref=src, dst_ref=dst, send_sem=send, recv_sem=recv,
        device_id={"blk": blk, "help": hlp}, device_id_type=MESH,
    )


def kernel(
    q_ref, kv_ref, sel_ref, own_ref, out_ref,
    kvl, vts, kbuf, vbuf, qbuf, sell, selv, sels, ownk, ownv, scores, part, stats, near, nstat,
    out_o, in_o, out_s, in_s,
    loc_sem, k_send, k_recv, f_send, f_recv,
    q_send, q_recv, s_send, s_recv, o_send, o_recv, t_send, t_recv,
):
    i = lax.axis_index("blk")
    j = lax.axis_index("help")
    g, u = i // 2, i % 2
    z, ylo = j // 2, j % 2
    me = 2 * g + ylo
    right = 2 * ((z + 1) % NZ) + ylo
    sib = 2 * g + (1 - u)

    def plane_of(t):
        return 2 * (t // 2) + u, 2 * z + t % 2

    barrier = pltpu.get_barrier_semaphore()

    def greet(b, h):
        pl.semaphore_signal(barrier, inc=1, device_id={"blk": b, "help": h}, device_id_type=MESH)

    lax.fori_loop(1, PLANE, lambda k, c: (greet(*plane_of((me + k) % PLANE)), c)[1], 0)
    lax.fori_loop(1, NZ, lambda k, c: (greet(i, 2 * ((z + k) % NZ) + ylo), c)[1], 0)
    greet(sib, j)

    gcol = pl.multiple_of(g * D, D)
    gval = pl.multiple_of(G * D + g * D, D)
    loads = [
        pltpu.make_async_copy(src, dst, loc_sem.at[n])
        for n, (src, dst) in enumerate((
            (kv_ref, kvl), (q_ref, qbuf.at[z]), (sel_ref.at[0], sell),
            (own_ref.at[:, pl.ds(gcol, D)], ownk), (own_ref.at[:, pl.ds(gval, D)], ownv),
        ))
    ]
    for copy in loads:
        copy.start()
    pl.semaphore_wait(barrier, PLANE - 1 + NZ - 1 + 1)

    def at(d):
        return (z + d + NZ) % NZ

    def q_piece(block, p):
        return qbuf.at[at(block), pl.ds(p * (R // PIECES), R // PIECES), :]

    def q_copy(way, s, p):
        hop = 2 if s == 4 else 1
        part_of = q_piece((s - hop) * (2 * way - 1), p)
        src = q_ref.at[pl.ds(p * (R // PIECES), R // PIECES), :] if s == 1 else part_of
        return remote(
            src, part_of, q_send.at[way, s - 1, p], q_recv.at[way, s - 1, p],
            i, 2 * at(hop * (1 - 2 * way)) + ylo,
        )

    def q_came(way, s, p):
        part_of = q_piece(s * (2 * way - 1), p)
        remote(part_of, part_of, q_send.at[way, s - 1, p], q_recv.at[way, s - 1, p], i, right).wait_recv()

    def q_steps(s):
        return [(w, p) for p in range(PIECES) for w in (0, 1) if s < 4 or p // (PIECES // 2) == w]

    def q_pass_on(s):
        for w, p in q_steps(s):
            q_came(w, s, p)
            if s == 2 and (w, p) in q_steps(4):
                q_copy(w, 4, p).start()
            q_copy(w, s + 1, p).start()

    for w, p in q_steps(1):
        q_copy(w, 1, p).start()
    for copy in loads:
        copy.wait()

    held = (kbuf, vbuf)

    def kv_copy(k, e):
        t = (me + k) % PLANE
        b, h = plane_of(t)
        src = vts.at[t // 2] if e else kvl.at[:, pl.ds(pl.multiple_of((t // 2) * D, D), D)]
        return remote(src, held[e].at[i, ylo], k_send.at[e, k], k_recv.at[e, me], b, h)

    def forward(s, e):
        block = held[e].at[2 * (s // 2) + u, s % 2]
        return remote(block, block, f_send.at[e, s], f_recv.at[e, s], sib, j)

    def s_copy(k):
        h = 2 * ((z + k) % NZ) + ylo
        return remote(selv.at[z], selv.at[z], s_send.at[k], s_recv.at[z], i, h)

    lax.fori_loop(1, PLANE, lambda k, c: (kv_copy(k, 0).start(), c)[1], 0)
    selv[z] = jnp.concatenate([sell[...], jnp.zeros((TOPK, D - sell.shape[1]), jnp.int32)], axis=1)
    lax.fori_loop(1, NZ, lambda k, c: (s_copy(k).start(), c)[1], 0)
    kbuf[i, ylo] = kvl[:, pl.ds(gcol, D)]
    forward(me, 0).start()
    for head in range(G):
        vts[head] = jnp.transpose(kvl[:, (G + head) * D : (G + head + 1) * D])
    vbuf[i, ylo] = vts[g]

    def arrive(e):
        def one(k, c):
            s = (me + PLANE - k) % PLANE
            block = held[e].at[2 * (s // 2) + u, s % 2]
            remote(block, block, k_send.at[e, k], k_recv.at[e, s], sib, j).wait_recv()
            forward(s, e).start()
            return c

        lax.fori_loop(1, PLANE, one, 0)

    def from_sibling(e):
        def one(s, c):
            block = held[e].at[2 * (s // 2) + (1 - u), s % 2]
            remote(block, block, f_send.at[e, s], f_recv.at[e, s], sib, j).wait_recv()
            return c

        lax.fori_loop(0, PLANE, one, 0)

    def picks_came(k, c):
        zs = (z + NZ - k) % NZ
        remote(selv.at[zs], selv.at[zs], s_send.at[k], s_recv.at[zs], i, right).wait_recv()
        return c

    q_pass_on(1)
    lax.fori_loop(1, PLANE, lambda k, c: (kv_copy(k, 1).start(), c)[1], 0)
    forward(me, 1).start()
    lax.fori_loop(1, NZ, picks_came, 0)
    to_smem = pltpu.make_async_copy(selv, sels, loc_sem.at[0])
    to_smem.start()
    q_pass_on(2)
    arrive(0)

    causal = lax.broadcasted_iota(jnp.int32, (R, R), 0) <= lax.broadcasted_iota(jnp.int32, (R, R), 1)
    own_vt = jnp.transpose(ownv[...])
    for h in range(HEADS):
        s = lax.dot_general(
            ownk[...], qbuf[z, :, h * D : (h + 1) * D], NT, preferred_element_type=jnp.float32
        )
        s = jnp.where(causal, s, FAR)
        top = jnp.max(s, axis=0, keepdims=True)
        w = jnp.exp2((s - top) * SCALE)
        nstat[h, 0:1] = top
        nstat[h, 1:2] = jnp.sum(w, axis=0, keepdims=True)
        near[h] = jnp.dot(own_vt, w.astype(jnp.bfloat16), preferred_element_type=jnp.float32)

    to_smem.wait()
    from_sibling(0)

    parity = z // (NZ // 2)
    lead = HEADS * i

    def score(b, carry):
        for h in range(HEADS):
            q = qbuf[b, :, h * D : (h + 1) * D]
            top = jnp.full((1, R), 4 * FAR, jnp.float32)
            for t in range(TOPK):
                c = sels[b, t, lead + h]
                k = kbuf[c // 2].reshape(2 * R, D)
                s = lax.dot_general(k, q, NT, preferred_element_type=jnp.float32)
                scores[b, h, t] = s
                bias = jnp.where(c % 2 == parity, 0.0, FAR)
                top = jnp.maximum(top, jnp.max(s, axis=0, keepdims=True) + bias)
            stats[b, h, 0:1] = top
        return carry

    lax.fori_loop(0, NZ - 3, lambda n, c: score((z + 6 + n) % NZ, c), 0)
    for s in (3, 4):
        for w, p in q_steps(s):
            q_came(w, s, p)
    arrive(1)
    lax.fori_loop(0, 3, lambda n, c: score((z + 3 + n) % NZ, c), 0)
    from_sibling(1)

    def attend(b, h):
        top = stats[b, h, 0:1]
        total = jnp.zeros((1, R), jnp.float32)
        acc = jnp.zeros((D, R), jnp.float32)
        for t in range(TOPK):
            c = sels[b, t, lead + h]
            level = jnp.where(c % 2 == parity, top * SCALE, -FAR)
            w = jnp.exp2(scores[b, h, t] * SCALE - level)
            total = total + jnp.sum(w, axis=0, keepdims=True)
            light = w.astype(jnp.bfloat16)
            for e in (0, 1):
                acc = acc + jnp.dot(
                    vbuf[c // 2, e], light[e * R : (e + 1) * R], preferred_element_type=jnp.float32
                )
        part[b, h] = acc
        stats[b, h, 1:2] = total

    def merge(a, b):
        (ma, la, oa), (mb, lb, ob) = a, b
        m = jnp.maximum(ma, mb)
        fa, fb = jnp.exp2((ma - m) * SCALE), jnp.exp2((mb - m) * SCALE)
        return m, la * fa + lb * fb, oa * fa + ob * fb

    def mine(b, h):
        return stats[b, h, 0:1], stats[b, h, 1:2], part[b, h]

    def came(way, s, h):
        return in_s[way, s, h, 0:1], in_s[way, s, h, 1:2], in_o[way, s, h].astype(jnp.float32)

    def back(way, s, h, hop=1):
        hlp = 2 * ((z + hop + (NZ - 2 * hop) * way) % NZ) + ylo
        return (
            remote(out_o.at[way, s, h], in_o.at[way, s, h], o_send.at[way, s, h], o_recv.at[way, s, h], i, hlp),
            remote(out_s.at[way, s, h], in_s.at[way, s, h], t_send.at[way, s, h], t_recv.at[way, s, h], i, hlp),
        )

    def landed(way, s, h):
        for copy in back(way, s, h):
            copy.wait_recv()

    def give(way, s, h, state, hop=1):
        out_s[way, s, h, 0:1] = state[0]
        out_s[way, s, h, 1:2] = state[1]
        out_o[way, s, h] = state[2].astype(jnp.bfloat16)
        for copy in back(way, s, h, hop):
            copy.start()

    def turn(m, carry):
        n, c = m // 2, m % 2
        s = (n + 1) // 2
        way = (n + 1) % 2
        b = jnp.where(n == NZ - 1, z, jnp.where(way == 0, z + 4 - s, z + 4 + s) % NZ)
        for e in (0, 1):
            attend(b, 2 * c + e)

        heads = (2 * c, 2 * c + 1)

        @pl.when(n == 0)
        def _():
            for h in heads:
                give(c, 0, h, mine(b, h), 2)

        @pl.when((n == 1) | (n == 2))
        def _():
            for h in heads:
                give(way, s, h, mine(b, h))

        @pl.when((n > 2) & (n < NZ - 1) & ((n > 4) | (c != way)))
        def _():
            for h in heads:
                landed(way, s - 1, h)
                give(way, s, h, merge(mine(b, h), came(way, s - 1, h)))

        @pl.when(((n == 3) | (n == 4)) & (c == way))
        def _():
            for h in heads:
                landed(way, 0, h)
                landed(way, 1, h)
                give(way, 2, h, merge(merge(mine(b, h), came(way, 0, h)), came(way, 1, h)))

        return carry

    lax.fori_loop(0, 2 * NZ, turn, 0)

    for h in range(HEADS):
        state = merge(mine(z, h), (nstat[h, 0:1], nstat[h, 1:2], near[h]))
        for way in (0, 1):
            landed(way, 3, h)
            state = merge(state, came(way, 3, h))
        out_ref[:, h * D : (h + 1) * D] = jnp.transpose(state[2] / state[1])

    for s in range(1, 5):
        for w, p in q_steps(s):
            q_copy(w, s, p).wait_send()
    for e in (0, 1):
        lax.fori_loop(1, PLANE, lambda k, c: (kv_copy(k, e).wait_send(), c)[1], 0)
        lax.fori_loop(0, PLANE, lambda k, c: (forward(k, e).wait_send(), c)[1], 0)
    lax.fori_loop(1, NZ, lambda k, c: (s_copy(k).wait_send(), c)[1], 0)
    for s in range(4):
        for way in (0, 1):
            for h in range(HEADS):
                if s > 0 or h // 2 == way:
                    for copy in back(way, s, h):
                        copy.wait_send()


def local(queries, query_key_value, cached_key_value, selected):
    bf16, f32 = jnp.bfloat16, jnp.float32
    dma = pltpu.SemaphoreType.DMA
    hbm = pl.BlockSpec(memory_space=pl.ANY)
    return pl.pallas_call(
        kernel,
        out_shape=jax.ShapeDtypeStruct((R, HEADS * D), f32),
        in_specs=[hbm, hbm, hbm, hbm],
        out_specs=pl.BlockSpec(memory_space=pltpu.VMEM),
        scratch_shapes=[
            pltpu.VMEM((R, 2 * G * D), bf16),
            pltpu.VMEM((G, D, R), bf16),
            pltpu.VMEM((PAIRS, 2, R, D), bf16),
            pltpu.VMEM((PAIRS, 2, D, R), bf16),
            pltpu.VMEM((NZ, R, HEADS * D), bf16),
            pltpu.VMEM((TOPK, PAIRS * HEADS), jnp.int32),
            pltpu.VMEM((NZ, TOPK, D), jnp.int32),
            pltpu.SMEM((NZ, TOPK, D), jnp.int32),
            pltpu.VMEM((R, D), bf16),
            pltpu.VMEM((R, D), bf16),
            pltpu.VMEM((NZ, HEADS, TOPK, 2 * R, R), f32),
            pltpu.VMEM((NZ, HEADS, D, R), f32),
            pltpu.VMEM((NZ, HEADS, 8, R), f32),
            pltpu.VMEM((HEADS, D, R), f32),
            pltpu.VMEM((HEADS, 8, R), f32),
            pltpu.VMEM((2, 4, HEADS, D, R), bf16),
            pltpu.VMEM((2, 4, HEADS, D, R), bf16),
            pltpu.VMEM((2, 4, HEADS, 8, R), f32),
            pltpu.VMEM((2, 4, HEADS, 8, R), f32),
            dma((5,)),
            dma((2, PLANE)), dma((2, PLANE)), dma((2, PLANE)), dma((2, PLANE)),
            dma((2, 4, PIECES)), dma((2, 4, PIECES)),
            dma((NZ,)), dma((NZ,)),
            dma((2, 4, HEADS)), dma((2, 4, HEADS)), dma((2, 4, HEADS)), dma((2, 4, HEADS)),
        ],
        compiler_params=pltpu.CompilerParams(
            collective_id=0, has_side_effects=True, vmem_limit_bytes=58 * 2**20
        ),
    )(queries, cached_key_value, jnp.transpose(selected, (0, 2, 1)), query_key_value)


def solution(mesh):
    in_specs = (P("help", "blk"), P("help", None), P(("blk", "help"), None), P("help", None, None))
    return jax.shard_map(
        local, mesh=mesh, in_specs=in_specs, out_specs=P("help", "blk"), check_vma=False
    )
```

```python
import math

import jax
import jax.numpy as jnp
from jax import lax
from jax.experimental import pallas as pl
from jax.experimental.pallas import tpu as pltpu
from jax.sharding import PartitionSpec as P

D = 128
R = 128
G = 8
NZ = 8
TOPK = 8
HEADS = 4
PLANE = 16
PIECES = 4
TAIL = 16
FAR = -1e9
SCALE = math.log2(math.e) / math.sqrt(D)
MESH = pl.DeviceIdType.MESH
NT = (((1,), (1,)), ((), ()))


def remote(src, dst, send, recv, blk, hlp):
    return pltpu.make_async_remote_copy(
        src_ref=src, dst_ref=dst, send_sem=send, recv_sem=recv,
        device_id={"blk": blk, "help": hlp}, device_id_type=MESH,
    )


def kernel(
    q_ref, kv_ref, sel_ref, own_ref, out_ref,
    kvl, vts, kbuf, vbuf, qbuf, sell, selv, sels, ownk, ownv, scores, part, stats, near, nstat,
    out_o, in_o,
    loc_sem, k_send, k_recv, f_send, f_recv,
    q_send, q_recv, s_send, s_recv, o_send, o_recv,
):
    i = lax.axis_index("blk")
    j = lax.axis_index("help")
    g, u = i // 2, i % 2
    z, ylo = j // 2, j % 2
    me = 2 * g + ylo
    right = 2 * ((z + 1) % NZ) + ylo
    sib = 2 * g + (1 - u)

    def plane_of(t):
        return 2 * (t // 2) + u, 2 * z + t % 2

    barrier = pltpu.get_barrier_semaphore()

    def greet(b, h):
        pl.semaphore_signal(barrier, inc=1, device_id={"blk": b, "help": h}, device_id_type=MESH)

    lax.fori_loop(1, PLANE, lambda k, c: (greet(*plane_of((me + k) % PLANE)), c)[1], 0)
    lax.fori_loop(1, NZ, lambda k, c: (greet(i, 2 * ((z + k) % NZ) + ylo), c)[1], 0)
    greet(sib, j)

    gcol = pl.multiple_of(g * D, D)
    gval = pl.multiple_of(G * D + g * D, D)
    loads = [
        pltpu.make_async_copy(src, dst, loc_sem.at[n])
        for n, (src, dst) in enumerate((
            (kv_ref, kvl), (q_ref, qbuf.at[z]), (sel_ref.at[0], sell),
            (own_ref.at[:, pl.ds(gcol, D)], ownk), (own_ref.at[:, pl.ds(gval, D)], ownv),
        ))
    ]
    for copy in loads:
        copy.start()
    pl.semaphore_wait(barrier, PLANE - 1 + NZ - 1 + 1)

    def at(d):
        return (z + d + NZ) % NZ

    def q_piece(block, p):
        return qbuf.at[at(block), pl.ds(p * (R // PIECES), R // PIECES), :]

    def q_copy(way, s, p):
        hop = 2 if s == 4 else 1
        part_of = q_piece((s - hop) * (2 * way - 1), p)
        src = q_ref.at[pl.ds(p * (R // PIECES), R // PIECES), :] if s == 1 else part_of
        return remote(
            src, part_of, q_send.at[way, s - 1, p], q_recv.at[way, s - 1, p],
            i, 2 * at(hop * (1 - 2 * way)) + ylo,
        )

    def q_came(way, s, p):
        part_of = q_piece(s * (2 * way - 1), p)
        remote(part_of, part_of, q_send.at[way, s - 1, p], q_recv.at[way, s - 1, p], i, right).wait_recv()

    def q_steps(s):
        return [(w, p) for p in range(PIECES) for w in (0, 1) if s < 4 or p // (PIECES // 2) == w]

    def q_pass_on(s):
        for w, p in q_steps(s):
            q_came(w, s, p)
            if s == 2 and (w, p) in q_steps(4):
                q_copy(w, 4, p).start()
            q_copy(w, s + 1, p).start()

    for w, p in q_steps(1):
        q_copy(w, 1, p).start()
    for copy in loads:
        copy.wait()

    held = (kbuf, vbuf)

    def kv_copy(k, e):
        t = (me + k) % PLANE
        b, h = plane_of(t)
        src = vts.at[t // 2] if e else kvl.at[:, pl.ds(pl.multiple_of((t // 2) * D, D), D)]
        return remote(src, held[e].at[g, u, ylo], k_send.at[e, k], k_recv.at[e, me], b, h)

    def forward(part_of, e):
        block = held[e].at[pl.ds(part_of * (G // 2), G // 2), u]
        return remote(block, block, f_send.at[e, part_of], f_recv.at[e, part_of], sib, j)

    def s_copy(k):
        h = 2 * ((z + k) % NZ) + ylo
        return remote(selv.at[z], selv.at[z], s_send.at[k], s_recv.at[z], i, h)

    lax.fori_loop(1, PLANE, lambda k, c: (kv_copy(k, 0).start(), c)[1], 0)
    selv[z] = jnp.concatenate([sell[...], jnp.zeros((TOPK, D - sell.shape[1]), jnp.int32)], axis=1)
    lax.fori_loop(1, NZ, lambda k, c: (s_copy(k).start(), c)[1], 0)
    kbuf[g, u, ylo] = kvl[:, pl.ds(gcol, D)]
    for head in range(G):
        vts[head] = jnp.transpose(kvl[:, (G + head) * D : (G + head + 1) * D])
    vbuf[g, u, ylo] = vts[g]

    def arrive(e):
        def one(s, c):
            @pl.when(s != me)
            def _():
                block = held[e].at[s // 2, u, s % 2]
                remote(block, block, k_send.at[e, 0], k_recv.at[e, s], sib, j).wait_recv()

            return c

        for part_of in (0, 1):
            lax.fori_loop(part_of * (PLANE // 2), (part_of + 1) * (PLANE // 2), one, 0)
            forward(part_of, e).start()

    def from_sibling(e):
        for part_of in (0, 1):
            block = held[e].at[pl.ds(part_of * (G // 2), G // 2), 1 - u]
            remote(block, block, f_send.at[e, part_of], f_recv.at[e, part_of], sib, j).wait_recv()

    def picks_came(k, c):
        zs = (z + NZ - k) % NZ
        remote(selv.at[zs], selv.at[zs], s_send.at[k], s_recv.at[zs], i, right).wait_recv()
        return c

    q_pass_on(1)
    lax.fori_loop(1, PLANE, lambda k, c: (kv_copy(k, 1).start(), c)[1], 0)
    lax.fori_loop(1, NZ, picks_came, 0)
    to_smem = pltpu.make_async_copy(selv, sels, loc_sem.at[0])
    to_smem.start()
    q_pass_on(2)
    arrive(0)

    causal = lax.broadcasted_iota(jnp.int32, (R, R), 0) <= lax.broadcasted_iota(jnp.int32, (R, R), 1)
    own_vt = jnp.transpose(ownv[...])
    for h in range(HEADS):
        s = lax.dot_general(
            ownk[...], qbuf[z, :, h * D : (h + 1) * D], NT, preferred_element_type=jnp.float32
        )
        s = jnp.where(causal, s, FAR)
        top = jnp.max(s, axis=0, keepdims=True)
        w = jnp.exp2((s - top) * SCALE)
        nstat[h, 0:1] = top
        nstat[h, 1:2] = jnp.sum(w, axis=0, keepdims=True)
        near[h] = jnp.dot(own_vt, w.astype(jnp.bfloat16), preferred_element_type=jnp.float32)

    to_smem.wait()
    from_sibling(0)

    parity = z // (NZ // 2)
    lead = HEADS * i

    def score(b, carry):
        for h in range(HEADS):
            q = qbuf[b, :, h * D : (h + 1) * D]
            top = jnp.full((1, R), 4 * FAR, jnp.float32)
            for t in range(TOPK):
                c = sels[b, t, lead + h]
                k = kbuf[c // 4, c // 2 % 2].reshape(2 * R, D)
                s = lax.dot_general(k, q, NT, preferred_element_type=jnp.float32)
                scores[b, h, t] = s
                bias = jnp.where(c % 2 == parity, 0.0, FAR)
                top = jnp.maximum(top, jnp.max(s, axis=0, keepdims=True) + bias)
            stats[b, h, 0:1] = top
        return carry

    lax.fori_loop(0, NZ - 3, lambda n, c: score((z + 6 + n) % NZ, c), 0)
    for s in (3, 4):
        for w, p in q_steps(s):
            q_came(w, s, p)
    arrive(1)
    lax.fori_loop(0, 3, lambda n, c: score((z + 3 + n) % NZ, c), 0)
    from_sibling(1)

    def attend(b, h):
        top = stats[b, h, 0:1]
        total = jnp.zeros((1, R), jnp.float32)
        acc = jnp.zeros((D, R), jnp.float32)
        for t in range(TOPK):
            c = sels[b, t, lead + h]
            level = jnp.where(c % 2 == parity, top * SCALE, -FAR)
            w = jnp.exp2(scores[b, h, t] * SCALE - level)
            total = total + jnp.sum(w, axis=0, keepdims=True)
            light = w.astype(jnp.bfloat16)
            for e in (0, 1):
                acc = acc + jnp.dot(
                    vbuf[c // 4, c // 2 % 2, e], light[e * R : (e + 1) * R], preferred_element_type=jnp.float32
                )
        part[b, h] = acc
        stats[b, h, 1:2] = total

    def merge(a, b):
        (ma, la, oa), (mb, lb, ob) = a, b
        m = jnp.maximum(ma, mb)
        fa, fb = jnp.exp2((ma - m) * SCALE), jnp.exp2((mb - m) * SCALE)
        return m, la * fa + lb * fb, oa * fa + ob * fb

    def mine(b, h):
        return stats[b, h, 0:1], stats[b, h, 1:2], part[b, h]

    def thirds(x):
        hi = x.astype(jnp.bfloat16).astype(jnp.float32)
        mid = (x - hi).astype(jnp.bfloat16).astype(jnp.float32)
        return [hi, mid, x - hi - mid]

    def came(way, s, h):
        rows = in_o[way, s, h, D:].astype(jnp.float32)
        return (
            rows[0:1] + rows[1:2] + rows[2:3], rows[3:4] + rows[4:5] + rows[5:6],
            in_o[way, s, h, :D].astype(jnp.float32),
        )

    def back(way, s, h, hop=1):
        hlp = 2 * ((z + hop + (NZ - 2 * hop) * way) % NZ) + ylo
        return remote(
            out_o.at[way, s, h], in_o.at[way, s, h], o_send.at[way, s, h], o_recv.at[way, s, h], i, hlp
        )

    def landed(way, s, h):
        back(way, s, h).wait_recv()

    def give(way, s, h, state, hop=1):
        rows = jnp.concatenate(thirds(state[0]) + thirds(state[1]) + [jnp.zeros((TAIL - 6, R), jnp.float32)], axis=0)
        out_o[way, s, h, :D] = state[2].astype(jnp.bfloat16)
        out_o[way, s, h, D:] = rows.astype(jnp.bfloat16)
        back(way, s, h, hop).start()

    def all_have_left():
        for s in range(1, 5):
            for w, p in q_steps(s):
                q_copy(w, s, p).wait_send()
        for e in (0, 1):
            lax.fori_loop(1, PLANE, lambda k, c: (kv_copy(k, e).wait_send(), c)[1], 0)
            for part_of in (0, 1):
                forward(part_of, e).wait_send()
        lax.fori_loop(1, NZ, lambda k, c: (s_copy(k).wait_send(), c)[1], 0)

    def turn(m, carry):
        n, c = m // 2, m % 2
        s = (n + 1) // 2
        way = (n + 1) % 2
        b = jnp.where(n == NZ - 1, z, jnp.where(way == 0, z + 4 - s, z + 4 + s) % NZ)
        for e in (0, 1):
            attend(b, 2 * c + e)

        heads = (2 * c, 2 * c + 1)

        @pl.when(m == 6)
        def _():
            all_have_left()

        @pl.when(n == 0)
        def _():
            for h in heads:
                give(c, 0, h, mine(b, h), 2)

        @pl.when((n == 1) | (n == 2))
        def _():
            for h in heads:
                give(way, s, h, mine(b, h))

        @pl.when((n > 2) & (n < NZ - 1) & ((n > 4) | (c != way)))
        def _():
            for h in heads:
                landed(way, s - 1, h)
                give(way, s, h, merge(mine(b, h), came(way, s - 1, h)))

        @pl.when(((n == 3) | (n == 4)) & (c == way))
        def _():
            for h in heads:
                landed(way, 0, h)
                landed(way, 1, h)
                give(way, 2, h, merge(merge(mine(b, h), came(way, 0, h)), came(way, 1, h)))

        return carry

    lax.fori_loop(0, 2 * NZ, turn, 0)

    for h in range(HEADS):
        state = merge(mine(z, h), (nstat[h, 0:1], nstat[h, 1:2], near[h]))
        for way in (0, 1):
            landed(way, 3, h)
            state = merge(state, came(way, 3, h))
        out_ref[:, h * D : (h + 1) * D] = jnp.transpose(state[2] / state[1])

    for s in range(4):
        for way in (0, 1):
            for h in range(HEADS):
                if s > 0 or h // 2 == way:
                    back(way, s, h).wait_send()


def local(queries, query_key_value, cached_key_value, selected):
    bf16, f32 = jnp.bfloat16, jnp.float32
    dma = pltpu.SemaphoreType.DMA
    hbm = pl.BlockSpec(memory_space=pl.ANY)
    return pl.pallas_call(
        kernel,
        out_shape=jax.ShapeDtypeStruct((R, HEADS * D), f32),
        in_specs=[hbm, hbm, hbm, hbm],
        out_specs=pl.BlockSpec(memory_space=pltpu.VMEM),
        scratch_shapes=[
            pltpu.VMEM((R, 2 * G * D), bf16),
            pltpu.VMEM((G, D, R), bf16),
            pltpu.VMEM((G, 2, 2, R, D), bf16),
            pltpu.VMEM((G, 2, 2, D, R), bf16),
            pltpu.VMEM((NZ, R, HEADS * D), bf16),
            pltpu.VMEM((TOPK, PLANE * HEADS), jnp.int32),
            pltpu.VMEM((NZ, TOPK, D), jnp.int32),
            pltpu.SMEM((NZ, TOPK, D), jnp.int32),
            pltpu.VMEM((R, D), bf16),
            pltpu.VMEM((R, D), bf16),
            pltpu.VMEM((NZ, HEADS, TOPK, 2 * R, R), f32),
            pltpu.VMEM((NZ, HEADS, D, R), f32),
            pltpu.VMEM((NZ, HEADS, 8, R), f32),
            pltpu.VMEM((HEADS, D, R), f32),
            pltpu.VMEM((HEADS, 8, R), f32),
            pltpu.VMEM((2, 4, HEADS, D + TAIL, R), bf16),
            pltpu.VMEM((2, 4, HEADS, D + TAIL, R), bf16),
            dma((5,)),
            dma((2, PLANE)), dma((2, PLANE)), dma((2, 2)), dma((2, 2)),
            dma((2, 4, PIECES)), dma((2, 4, PIECES)),
            dma((NZ,)), dma((NZ,)),
            dma((2, 4, HEADS)), dma((2, 4, HEADS)),
        ],
        compiler_params=pltpu.CompilerParams(
            collective_id=0, has_side_effects=True, vmem_limit_bytes=58 * 2**20
        ),
    )(queries, cached_key_value, jnp.transpose(selected, (0, 2, 1)), query_key_value)


def solution(mesh):
    in_specs = (P("help", "blk"), P("help", None), P(("blk", "help"), None), P("help", None, None))
    return jax.shard_map(
        local, mesh=mesh, in_specs=in_specs, out_specs=P("help", "blk"), check_vma=False
    )
```

```python
import math

import jax
import jax.numpy as jnp
from jax import lax
from jax.experimental import pallas as pl
from jax.experimental.pallas import tpu as pltpu
from jax.sharding import PartitionSpec as P

D = 128
R = 128
G = 8
NZ = 8
TOPK = 8
HEADS = 4
PLANE = 16
PIECES = 4
TAIL = 16
FAR = -1e9
SCALE = math.log2(math.e) / math.sqrt(D)
MESH = pl.DeviceIdType.MESH
NT = (((1,), (1,)), ((), ()))


def remote(src, dst, send, recv, blk, hlp):
    return pltpu.make_async_remote_copy(
        src_ref=src, dst_ref=dst, send_sem=send, recv_sem=recv,
        device_id={"blk": blk, "help": hlp}, device_id_type=MESH,
    )


def kernel(
    q_ref, kv_ref, sel_ref, own_ref, out_ref,
    kvl, vts, kbuf, vbuf, qbuf, sell, selv, sels, ownk, ownv, scores, part, stats, near, nstat,
    out_o, in_o,
    loc_sem, k_send, k_recv, f_send, f_recv,
    q_send, q_recv, s_send, s_recv, o_send, o_recv,
):
    i = lax.axis_index("blk")
    j = lax.axis_index("help")
    g, u = i // 2, i % 2
    z, ylo = j // 2, j % 2
    me = 2 * g + ylo
    right = 2 * ((z + 1) % NZ) + ylo
    sib = 2 * g + (1 - u)

    def plane_of(t):
        return 2 * (t // 2) + u, 2 * z + t % 2

    barrier = pltpu.get_barrier_semaphore()

    def greet(b, h):
        pl.semaphore_signal(barrier, inc=1, device_id={"blk": b, "help": h}, device_id_type=MESH)

    lax.fori_loop(1, PLANE, lambda k, c: (greet(*plane_of((me + k) % PLANE)), c)[1], 0)
    lax.fori_loop(1, NZ, lambda k, c: (greet(i, 2 * ((z + k) % NZ) + ylo), c)[1], 0)
    greet(sib, j)

    gcol = pl.multiple_of(g * D, D)
    gval = pl.multiple_of(G * D + g * D, D)
    loads = [
        pltpu.make_async_copy(src, dst, loc_sem.at[n])
        for n, (src, dst) in enumerate((
            (kv_ref, kvl), (q_ref, qbuf.at[z]), (sel_ref.at[0], sell),
            (own_ref.at[:, pl.ds(gcol, D)], ownk), (own_ref.at[:, pl.ds(gval, D)], ownv),
        ))
    ]
    for copy in loads:
        copy.start()
    pl.semaphore_wait(barrier, PLANE - 1 + NZ - 1 + 1)

    def at(d):
        return (z + d + NZ) % NZ

    def q_piece(block, p):
        return qbuf.at[at(block), pl.ds(p * (R // PIECES), R // PIECES), :]

    def q_copy(way, s, p):
        hop = 2 if s == 4 else 1
        part_of = q_piece((s - hop) * (2 * way - 1), p)
        src = q_ref.at[pl.ds(p * (R // PIECES), R // PIECES), :] if s == 1 else part_of
        return remote(
            src, part_of, q_send.at[way, s - 1, p], q_recv.at[way, s - 1, p],
            i, 2 * at(hop * (1 - 2 * way)) + ylo,
        )

    def q_came(way, s, p):
        part_of = q_piece(s * (2 * way - 1), p)
        remote(part_of, part_of, q_send.at[way, s - 1, p], q_recv.at[way, s - 1, p], i, right).wait_recv()

    def q_steps(s):
        return [(w, p) for p in range(PIECES) for w in (0, 1) if s < 4 or p // (PIECES // 2) == w]

    def q_pass_on(s):
        for w, p in q_steps(s):
            q_came(w, s, p)
            if s == 2 and (w, p) in q_steps(4):
                q_copy(w, 4, p).start()
            q_copy(w, s + 1, p).start()

    for w, p in q_steps(1):
        q_copy(w, 1, p).start()
    for copy in loads:
        copy.wait()

    held = (kbuf, vbuf)

    def kv_copy(k, e):
        t = (me + k) % PLANE
        b, h = plane_of(t)
        src = vts.at[t // 2] if e else kvl.at[:, pl.ds(pl.multiple_of((t // 2) * D, D), D)]
        return remote(src, held[e].at[g, u, ylo], k_send.at[e, k], k_recv.at[e, me], b, h)

    def forward(part_of, e):
        block = held[e].at[pl.ds(part_of * (G // 2), G // 2), u]
        return remote(block, block, f_send.at[e, part_of], f_recv.at[e, part_of], sib, j)

    def s_copy(k):
        h = 2 * ((z + k) % NZ) + ylo
        return remote(selv.at[z], selv.at[z], s_send.at[k], s_recv.at[z], i, h)

    lax.fori_loop(1, PLANE, lambda k, c: (kv_copy(k, 0).start(), c)[1], 0)
    selv[z] = jnp.concatenate([sell[...], jnp.zeros((TOPK, D - sell.shape[1]), jnp.int32)], axis=1)
    lax.fori_loop(1, NZ, lambda k, c: (s_copy(k).start(), c)[1], 0)
    kbuf[g, u, ylo] = kvl[:, pl.ds(gcol, D)]
    for head in range(G):
        vts[head] = jnp.transpose(kvl[:, (G + head) * D : (G + head + 1) * D])
    vbuf[g, u, ylo] = vts[g]

    def arrive(e):
        def one(s, c):
            @pl.when(s != me)
            def _():
                block = held[e].at[s // 2, u, s % 2]
                remote(block, block, k_send.at[e, 0], k_recv.at[e, s], sib, j).wait_recv()

            return c

        for part_of in (0, 1):
            lax.fori_loop(part_of * (PLANE // 2), (part_of + 1) * (PLANE // 2), one, 0)
            forward(part_of, e).start()

    def from_sibling(e):
        for part_of in (0, 1):
            block = held[e].at[pl.ds(part_of * (G // 2), G // 2), 1 - u]
            remote(block, block, f_send.at[e, part_of], f_recv.at[e, part_of], sib, j).wait_recv()

    def picks_came(k, c):
        zs = (z + NZ - k) % NZ
        remote(selv.at[zs], selv.at[zs], s_send.at[k], s_recv.at[zs], i, right).wait_recv()
        return c

    q_pass_on(1)
    lax.fori_loop(1, NZ, picks_came, 0)
    to_smem = pltpu.make_async_copy(selv, sels, loc_sem.at[0])
    to_smem.start()
    q_pass_on(2)
    lax.fori_loop(1, PLANE, lambda k, c: (kv_copy(k, 1).start(), c)[1], 0)
    arrive(0)

    causal = lax.broadcasted_iota(jnp.int32, (R, R), 0) <= lax.broadcasted_iota(jnp.int32, (R, R), 1)
    own_vt = jnp.transpose(ownv[...])
    for h in range(HEADS):
        s = lax.dot_general(
            ownk[...], qbuf[z, :, h * D : (h + 1) * D], NT, preferred_element_type=jnp.float32
        )
        s = jnp.where(causal, s, FAR)
        top = jnp.max(s, axis=0, keepdims=True)
        w = jnp.exp2((s - top) * SCALE)
        nstat[h, 0:1] = top
        nstat[h, 1:2] = jnp.sum(w, axis=0, keepdims=True)
        near[h] = jnp.dot(own_vt, w.astype(jnp.bfloat16), preferred_element_type=jnp.float32)

    to_smem.wait()
    from_sibling(0)

    parity = z // (NZ // 2)
    lead = HEADS * i

    def score(b, carry):
        for h in range(HEADS):
            q = qbuf[b, :, h * D : (h + 1) * D]
            top = jnp.full((1, R), 4 * FAR, jnp.float32)
            for t in range(TOPK):
                c = sels[b, t, lead + h]
                k = kbuf[c // 4, c // 2 % 2].reshape(2 * R, D)
                s = lax.dot_general(k, q, NT, preferred_element_type=jnp.float32)
                scores[b, h, t] = s
                bias = jnp.where(c % 2 == parity, 0.0, FAR)
                top = jnp.maximum(top, jnp.max(s, axis=0, keepdims=True) + bias)
            stats[b, h, 0:1] = top
        return carry

    lax.fori_loop(0, NZ - 3, lambda n, c: score((z + 6 + n) % NZ, c), 0)
    for s in (3, 4):
        for w, p in q_steps(s):
            q_came(w, s, p)
    arrive(1)
    lax.fori_loop(0, 3, lambda n, c: score((z + 3 + n) % NZ, c), 0)
    from_sibling(1)

    def attend(b, h):
        top = stats[b, h, 0:1]
        total = jnp.zeros((1, R), jnp.float32)
        acc = jnp.zeros((D, R), jnp.float32)
        for t in range(TOPK):
            c = sels[b, t, lead + h]
            level = jnp.where(c % 2 == parity, top * SCALE, -FAR)
            w = jnp.exp2(scores[b, h, t] * SCALE - level)
            total = total + jnp.sum(w, axis=0, keepdims=True)
            light = w.astype(jnp.bfloat16)
            for e in (0, 1):
                acc = acc + jnp.dot(
                    vbuf[c // 4, c // 2 % 2, e], light[e * R : (e + 1) * R], preferred_element_type=jnp.float32
                )
        part[b, h] = acc
        stats[b, h, 1:2] = total

    def merge(a, b):
        (ma, la, oa), (mb, lb, ob) = a, b
        m = jnp.maximum(ma, mb)
        fa, fb = jnp.exp2((ma - m) * SCALE), jnp.exp2((mb - m) * SCALE)
        return m, la * fa + lb * fb, oa * fa + ob * fb

    def mine(b, h):
        return stats[b, h, 0:1], stats[b, h, 1:2], part[b, h]

    def thirds(x):
        hi = x.astype(jnp.bfloat16).astype(jnp.float32)
        mid = (x - hi).astype(jnp.bfloat16).astype(jnp.float32)
        return [hi, mid, x - hi - mid]

    def came(way, s, h):
        rows = in_o[way, s, h, D:].astype(jnp.float32)
        return (
            rows[0:1] + rows[1:2] + rows[2:3], rows[3:4] + rows[4:5] + rows[5:6],
            in_o[way, s, h, :D].astype(jnp.float32),
        )

    def back(way, s, h, hop=1):
        hlp = 2 * ((z + hop + (NZ - 2 * hop) * way) % NZ) + ylo
        return remote(
            out_o.at[way, s, h], in_o.at[way, s, h], o_send.at[way, s, h], o_recv.at[way, s, h], i, hlp
        )

    def landed(way, s, h):
        back(way, s, h).wait_recv()

    def give(way, s, h, state, hop=1):
        rows = jnp.concatenate(thirds(state[0]) + thirds(state[1]) + [jnp.zeros((TAIL - 6, R), jnp.float32)], axis=0)
        out_o[way, s, h, :D] = state[2].astype(jnp.bfloat16)
        out_o[way, s, h, D:] = rows.astype(jnp.bfloat16)
        back(way, s, h, hop).start()

    def all_have_left():
        for s in range(1, 5):
            for w, p in q_steps(s):
                q_copy(w, s, p).wait_send()
        for e in (0, 1):
            lax.fori_loop(1, PLANE, lambda k, c: (kv_copy(k, e).wait_send(), c)[1], 0)
            for part_of in (0, 1):
                forward(part_of, e).wait_send()
        lax.fori_loop(1, NZ, lambda k, c: (s_copy(k).wait_send(), c)[1], 0)

    def turn(m, carry):
        n, c = m // 2, m % 2
        s = (n + 1) // 2
        way = (n + 1) % 2
        b = jnp.where(n == NZ - 1, z, jnp.where(way == 0, z + 4 - s, z + 4 + s) % NZ)
        for e in (0, 1):
            attend(b, 2 * c + e)

        heads = (2 * c, 2 * c + 1)

        @pl.when(m == 6)
        def _():
            all_have_left()

        @pl.when(n == 0)
        def _():
            for h in heads:
                give(c, 0, h, mine(b, h), 2)

        @pl.when((n == 1) | (n == 2))
        def _():
            for h in heads:
                give(way, s, h, mine(b, h))

        @pl.when((n > 2) & (n < NZ - 1) & ((n > 4) | (c != way)))
        def _():
            for h in heads:
                landed(way, s - 1, h)
                give(way, s, h, merge(mine(b, h), came(way, s - 1, h)))

        @pl.when(((n == 3) | (n == 4)) & (c == way))
        def _():
            for h in heads:
                landed(way, 0, h)
                landed(way, 1, h)
                give(way, 2, h, merge(merge(mine(b, h), came(way, 0, h)), came(way, 1, h)))

        return carry

    lax.fori_loop(0, 2 * NZ, turn, 0)

    for h in range(HEADS):
        state = merge(mine(z, h), (nstat[h, 0:1], nstat[h, 1:2], near[h]))
        for way in (0, 1):
            landed(way, 3, h)
            state = merge(state, came(way, 3, h))
        out_ref[:, h * D : (h + 1) * D] = jnp.transpose(state[2] / state[1])

    for s in range(4):
        for way in (0, 1):
            for h in range(HEADS):
                if s > 0 or h // 2 == way:
                    back(way, s, h).wait_send()


def local(queries, query_key_value, cached_key_value, selected):
    bf16, f32 = jnp.bfloat16, jnp.float32
    dma = pltpu.SemaphoreType.DMA
    hbm = pl.BlockSpec(memory_space=pl.ANY)
    return pl.pallas_call(
        kernel,
        out_shape=jax.ShapeDtypeStruct((R, HEADS * D), f32),
        in_specs=[hbm, hbm, hbm, hbm],
        out_specs=pl.BlockSpec(memory_space=pltpu.VMEM),
        scratch_shapes=[
            pltpu.VMEM((R, 2 * G * D), bf16),
            pltpu.VMEM((G, D, R), bf16),
            pltpu.VMEM((G, 2, 2, R, D), bf16),
            pltpu.VMEM((G, 2, 2, D, R), bf16),
            pltpu.VMEM((NZ, R, HEADS * D), bf16),
            pltpu.VMEM((TOPK, PLANE * HEADS), jnp.int32),
            pltpu.VMEM((NZ, TOPK, D), jnp.int32),
            pltpu.SMEM((NZ, TOPK, D), jnp.int32),
            pltpu.VMEM((R, D), bf16),
            pltpu.VMEM((R, D), bf16),
            pltpu.VMEM((NZ, HEADS, TOPK, 2 * R, R), f32),
            pltpu.VMEM((NZ, HEADS, D, R), f32),
            pltpu.VMEM((NZ, HEADS, 8, R), f32),
            pltpu.VMEM((HEADS, D, R), f32),
            pltpu.VMEM((HEADS, 8, R), f32),
            pltpu.VMEM((2, 4, HEADS, D + TAIL, R), bf16),
            pltpu.VMEM((2, 4, HEADS, D + TAIL, R), bf16),
            dma((5,)),
            dma((2, PLANE)), dma((2, PLANE)), dma((2, 2)), dma((2, 2)),
            dma((2, 4, PIECES)), dma((2, 4, PIECES)),
            dma((NZ,)), dma((NZ,)),
            dma((2, 4, HEADS)), dma((2, 4, HEADS)),
        ],
        compiler_params=pltpu.CompilerParams(
            collective_id=0, has_side_effects=True, vmem_limit_bytes=58 * 2**20
        ),
    )(queries, cached_key_value, jnp.transpose(selected, (0, 2, 1)), query_key_value)


def solution(mesh):
    in_specs = (P("help", "blk"), P("help", None), P(("blk", "help"), None), P("help", None, None))
    return jax.shard_map(
        local, mesh=mesh, in_specs=in_specs, out_specs=P("help", "blk"), check_vma=False
    )
```

```python
import math

import jax
import jax.numpy as jnp
from jax import lax
from jax.experimental import pallas as pl
from jax.experimental.pallas import tpu as pltpu
from jax.sharding import PartitionSpec as P

D = 128
R = 128
G = 8
NZ = 8
TOPK = 8
HEADS = 4
PLANE = 16
PIECES = 8
TAIL = 16
FAR = -1e9
SCALE = math.log2(math.e) / math.sqrt(D)
MESH = pl.DeviceIdType.MESH
NT = (((1,), (1,)), ((), ()))


def remote(src, dst, send, recv, blk, hlp):
    return pltpu.make_async_remote_copy(
        src_ref=src, dst_ref=dst, send_sem=send, recv_sem=recv,
        device_id={"blk": blk, "help": hlp}, device_id_type=MESH,
    )


def kernel(
    q_ref, kv_ref, sel_ref, own_ref, out_ref,
    kvl, vts, kbuf, vbuf, qbuf, sell, selv, sels, ownk, ownv, scores, part, stats, near, nstat,
    out_o, in_o,
    loc_sem, k_send, k_recv, f_send, f_recv,
    q_send, q_recv, s_send, s_recv, o_send, o_recv,
):
    i = lax.axis_index("blk")
    j = lax.axis_index("help")
    g, u = i // 2, i % 2
    z, ylo = j // 2, j % 2
    me = 2 * g + ylo
    right = 2 * ((z + 1) % NZ) + ylo
    sib = 2 * g + (1 - u)

    def plane_of(t):
        return 2 * (t // 2) + u, 2 * z + t % 2

    barrier = pltpu.get_barrier_semaphore()

    def greet(b, h):
        pl.semaphore_signal(barrier, inc=1, device_id={"blk": b, "help": h}, device_id_type=MESH)

    lax.fori_loop(1, PLANE, lambda k, c: (greet(*plane_of((me + k) % PLANE)), c)[1], 0)
    lax.fori_loop(1, NZ, lambda k, c: (greet(i, 2 * ((z + k) % NZ) + ylo), c)[1], 0)
    greet(sib, j)

    gcol = pl.multiple_of(g * D, D)
    gval = pl.multiple_of(G * D + g * D, D)
    loads = [
        pltpu.make_async_copy(src, dst, loc_sem.at[n])
        for n, (src, dst) in enumerate((
            (kv_ref, kvl), (q_ref, qbuf.at[z]), (sel_ref.at[0], sell),
            (own_ref.at[:, pl.ds(gcol, D)], ownk), (own_ref.at[:, pl.ds(gval, D)], ownv),
        ))
    ]
    for copy in loads:
        copy.start()
    pl.semaphore_wait(barrier, PLANE - 1 + NZ - 1 + 1)

    def at(d):
        return (z + d + NZ) % NZ

    def q_piece(block, p):
        return qbuf.at[at(block), pl.ds(p * (R // PIECES), R // PIECES), :]

    def q_copy(way, s, p):
        hop = 2 if s == 4 else 1
        part_of = q_piece((s - hop) * (2 * way - 1), p)
        src = q_ref.at[pl.ds(p * (R // PIECES), R // PIECES), :] if s == 1 else part_of
        return remote(
            src, part_of, q_send.at[way, s - 1, p], q_recv.at[way, s - 1, p],
            i, 2 * at(hop * (1 - 2 * way)) + ylo,
        )

    def q_came(way, s, p):
        part_of = q_piece(s * (2 * way - 1), p)
        remote(part_of, part_of, q_send.at[way, s - 1, p], q_recv.at[way, s - 1, p], i, right).wait_recv()

    def q_steps(s):
        return [(w, p) for p in range(PIECES) for w in (0, 1) if s < 4 or p // (PIECES // 2) == w]

    def q_pass_on(s):
        for w, p in q_steps(s):
            q_came(w, s, p)
            if s == 2 and (w, p) in q_steps(4):
                q_copy(w, 4, p).start()
            q_copy(w, s + 1, p).start()

    for w, p in q_steps(1):
        q_copy(w, 1, p).start()
    for copy in loads:
        copy.wait()

    held = (kbuf, vbuf)

    def kv_copy(k, e):
        t = (me + k) % PLANE
        b, h = plane_of(t)
        src = vts.at[t // 2] if e else kvl.at[:, pl.ds(pl.multiple_of((t // 2) * D, D), D)]
        return remote(src, held[e].at[g, u, ylo], k_send.at[e, k], k_recv.at[e, me], b, h)

    def forward(part_of, e):
        block = held[e].at[pl.ds(part_of * (G // 2), G // 2), u]
        return remote(block, block, f_send.at[e, part_of], f_recv.at[e, part_of], sib, j)

    def s_copy(k):
        h = 2 * ((z + k) % NZ) + ylo
        return remote(selv.at[z], selv.at[z], s_send.at[k], s_recv.at[z], i, h)

    lax.fori_loop(1, PLANE, lambda k, c: (kv_copy(k, 0).start(), c)[1], 0)
    selv[z] = jnp.concatenate([sell[...], jnp.zeros((TOPK, D - sell.shape[1]), jnp.int32)], axis=1)
    lax.fori_loop(1, NZ, lambda k, c: (s_copy(k).start(), c)[1], 0)
    kbuf[g, u, ylo] = kvl[:, pl.ds(gcol, D)]
    for head in range(G):
        vts[head] = jnp.transpose(kvl[:, (G + head) * D : (G + head + 1) * D])
    vbuf[g, u, ylo] = vts[g]

    def arrive(e):
        def one(s, c):
            @pl.when(s != me)
            def _():
                block = held[e].at[s // 2, u, s % 2]
                remote(block, block, k_send.at[e, 0], k_recv.at[e, s], sib, j).wait_recv()

            return c

        for part_of in (0, 1):
            lax.fori_loop(part_of * (PLANE // 2), (part_of + 1) * (PLANE // 2), one, 0)
            forward(part_of, e).start()

    def from_sibling(e):
        for part_of in (0, 1):
            block = held[e].at[pl.ds(part_of * (G // 2), G // 2), 1 - u]
            remote(block, block, f_send.at[e, part_of], f_recv.at[e, part_of], sib, j).wait_recv()

    def picks_came(k, c):
        zs = (z + NZ - k) % NZ
        remote(selv.at[zs], selv.at[zs], s_send.at[k], s_recv.at[zs], i, right).wait_recv()
        return c

    q_pass_on(1)
    lax.fori_loop(1, NZ, picks_came, 0)
    to_smem = pltpu.make_async_copy(selv, sels, loc_sem.at[0])
    to_smem.start()
    q_pass_on(2)
    lax.fori_loop(1, PLANE, lambda k, c: (kv_copy(k, 1).start(), c)[1], 0)
    arrive(0)

    causal = lax.broadcasted_iota(jnp.int32, (R, R), 0) <= lax.broadcasted_iota(jnp.int32, (R, R), 1)
    own_vt = jnp.transpose(ownv[...])
    for h in range(HEADS):
        s = lax.dot_general(
            ownk[...], qbuf[z, :, h * D : (h + 1) * D], NT, preferred_element_type=jnp.float32
        )
        s = jnp.where(causal, s * SCALE, FAR)
        top = jnp.max(s, axis=0, keepdims=True)
        w = jnp.exp2(s - top)
        nstat[h, 0:1] = top
        nstat[h, 1:2] = jnp.sum(w, axis=0, keepdims=True)
        near[h] = jnp.dot(own_vt, w.astype(jnp.bfloat16), preferred_element_type=jnp.float32)

    to_smem.wait()
    from_sibling(0)

    parity = z // (NZ // 2)
    lead = HEADS * i

    def score(b, carry):
        for h in range(HEADS):
            q = qbuf[b, :, h * D : (h + 1) * D]
            top = jnp.full((8, R), 4 * FAR, jnp.float32)
            for t in range(TOPK):
                c = sels[b, t, lead + h]
                k = kbuf[c // 4, c // 2 % 2].reshape(2 * R, D)
                s = lax.dot_general(k, q, NT, preferred_element_type=jnp.float32) * SCALE
                scores[b, h, t] = s
                bias = jnp.where(c % 2 == parity, 0.0, FAR)
                top = jnp.maximum(top, jnp.max(s.reshape(2 * R // 8, 8, R), axis=0) + bias)
            stats[b, h, 0:1] = jnp.max(top, axis=0, keepdims=True)
        return carry

    lax.fori_loop(0, NZ - 3, lambda n, c: score((z + 6 + n) % NZ, c), 0)
    for s in (3, 4):
        for w, p in q_steps(s):
            q_came(w, s, p)
    arrive(1)
    lax.fori_loop(0, 3, lambda n, c: score((z + 3 + n) % NZ, c), 0)
    from_sibling(1)

    def attend(b, h):
        top = stats[b, h, 0:1]
        total = jnp.zeros((8, R), jnp.float32)
        acc = jnp.zeros((D, R), jnp.float32)
        for t in range(TOPK):
            c = sels[b, t, lead + h]
            level = jnp.where(c % 2 == parity, top, -FAR)
            w = jnp.exp2(scores[b, h, t] - level)
            total = total + jnp.sum(w.reshape(2 * R // 8, 8, R), axis=0)
            light = w.astype(jnp.bfloat16)
            for e in (0, 1):
                acc = acc + jnp.dot(
                    vbuf[c // 4, c // 2 % 2, e], light[e * R : (e + 1) * R], preferred_element_type=jnp.float32
                )
        part[b, h] = acc
        stats[b, h, 1:2] = jnp.sum(total, axis=0, keepdims=True)

    def merge(a, b):
        (ma, la, oa), (mb, lb, ob) = a, b
        m = jnp.maximum(ma, mb)
        fa, fb = jnp.exp2(ma - m), jnp.exp2(mb - m)
        return m, la * fa + lb * fb, oa * fa + ob * fb

    def mine(b, h):
        return stats[b, h, 0:1], stats[b, h, 1:2], part[b, h]

    def thirds(x):
        hi = x.astype(jnp.bfloat16).astype(jnp.float32)
        mid = (x - hi).astype(jnp.bfloat16).astype(jnp.float32)
        return [hi, mid, x - hi - mid]

    def keep(h, state):
        stats[z, h, 0:1], stats[z, h, 1:2], part[z, h] = state

    def came(way, s, h):
        rows = in_o[way, s, h, D:].astype(jnp.float32)
        return (
            rows[0:1] + rows[1:2] + rows[2:3], rows[3:4] + rows[4:5] + rows[5:6],
            in_o[way, s, h, :D].astype(jnp.float32),
        )

    def back(way, s, h, hop=1):
        hlp = 2 * ((z + hop + (NZ - 2 * hop) * way) % NZ) + ylo
        return remote(
            out_o.at[way, s, h], in_o.at[way, s, h], o_send.at[way, s, h], o_recv.at[way, s, h], i, hlp
        )

    def landed(way, s, h):
        back(way, s, h).wait_recv()

    def give(way, s, h, state, hop=1):
        rows = jnp.concatenate(thirds(state[0]) + thirds(state[1]) + [jnp.zeros((TAIL - 6, R), jnp.float32)], axis=0)
        out_o[way, s, h, :D] = state[2].astype(jnp.bfloat16)
        out_o[way, s, h, D:] = rows.astype(jnp.bfloat16)
        back(way, s, h, hop).start()

    def all_have_left():
        for s in range(1, 5):
            for w, p in q_steps(s):
                q_copy(w, s, p).wait_send()
        for e in (0, 1):
            lax.fori_loop(1, PLANE, lambda k, c: (kv_copy(k, e).wait_send(), c)[1], 0)
            for part_of in (0, 1):
                forward(part_of, e).wait_send()
        lax.fori_loop(1, NZ, lambda k, c: (s_copy(k).wait_send(), c)[1], 0)

    def turn(m, carry):
        n, c = m // 2, m % 2
        s = (n + 1) // 2
        way = (n + 1) % 2
        b = jnp.where(way == 0, z + 4 - s, z + 4 + s) % NZ
        heads = (2 * c, 2 * c + 1)
        for h in heads:
            attend(b, h)

        @pl.when(n == 0)
        def _():
            for h in heads:
                give(c, 0, h, mine(b, h), 2)

        @pl.when((n == 1) | (n == 2))
        def _():
            for h in heads:
                give(way, s, h, mine(b, h))

        return carry

    lax.fori_loop(0, 2 * (NZ - 1), turn, 0)
    all_have_left()
    for h in range(HEADS):
        for way in (0, 1):
            b = at((2 - 4 * way))
            state = mine(b, h)
            if h // 2 == way:
                landed(way, 0, h)
                state = merge(state, came(way, 0, h))
            landed(way, 1, h)
            give(way, 2, h, merge(state, came(way, 1, h)))
    lax.fori_loop(0, HEADS, lambda h, c: (attend(z, h), c)[1], 0)
    for h in range(HEADS):
        keep(h, merge(mine(z, h), (nstat[h, 0:1], nstat[h, 1:2], near[h])))
    for h in range(HEADS):
        for way in (0, 1):
            landed(way, 2, h)
            give(way, 3, h, merge(mine(at(1 - 2 * way), h), came(way, 2, h)))

    for h in range(HEADS):
        state = mine(z, h)
        for way in (0, 1):
            landed(way, 3, h)
            state = merge(state, came(way, 3, h))
        out_ref[:, h * D : (h + 1) * D] = jnp.transpose(state[2] / state[1])

    for s in range(4):
        for way in (0, 1):
            for h in range(HEADS):
                if s > 0 or h // 2 == way:
                    back(way, s, h).wait_send()


def local(queries, query_key_value, cached_key_value, selected):
    bf16, f32 = jnp.bfloat16, jnp.float32
    dma = pltpu.SemaphoreType.DMA
    hbm = pl.BlockSpec(memory_space=pl.ANY)
    return pl.pallas_call(
        kernel,
        out_shape=jax.ShapeDtypeStruct((R, HEADS * D), f32),
        in_specs=[hbm, hbm, hbm, hbm],
        out_specs=pl.BlockSpec(memory_space=pltpu.VMEM),
        scratch_shapes=[
            pltpu.VMEM((R, 2 * G * D), bf16),
            pltpu.VMEM((G, D, R), bf16),
            pltpu.VMEM((G, 2, 2, R, D), bf16),
            pltpu.VMEM((G, 2, 2, D, R), bf16),
            pltpu.VMEM((NZ, R, HEADS * D), bf16),
            pltpu.VMEM((TOPK, PLANE * HEADS), jnp.int32),
            pltpu.VMEM((NZ, TOPK, D), jnp.int32),
            pltpu.SMEM((NZ, TOPK, D), jnp.int32),
            pltpu.VMEM((R, D), bf16),
            pltpu.VMEM((R, D), bf16),
            pltpu.VMEM((NZ, HEADS, TOPK, 2 * R, R), f32),
            pltpu.VMEM((NZ, HEADS, D, R), f32),
            pltpu.VMEM((NZ, HEADS, 8, R), f32),
            pltpu.VMEM((HEADS, D, R), f32),
            pltpu.VMEM((HEADS, 8, R), f32),
            pltpu.VMEM((2, 4, HEADS, D + TAIL, R), bf16),
            pltpu.VMEM((2, 4, HEADS, D + TAIL, R), bf16),
            dma((5,)),
            dma((2, PLANE)), dma((2, PLANE)), dma((2, 2)), dma((2, 2)),
            dma((2, 4, PIECES)), dma((2, 4, PIECES)),
            dma((NZ,)), dma((NZ,)),
            dma((2, 4, HEADS)), dma((2, 4, HEADS)),
        ],
        compiler_params=pltpu.CompilerParams(
            collective_id=0, has_side_effects=True, vmem_limit_bytes=58 * 2**20
        ),
    )(queries, cached_key_value, jnp.transpose(selected, (0, 2, 1)), query_key_value)


def solution(mesh):
    in_specs = (P("help", "blk"), P("help", None), P(("blk", "help"), None), P("help", None, None))
    return jax.shard_map(
        local, mesh=mesh, in_specs=in_specs, out_specs=P("help", "blk"), check_vma=False
    )
```
